512 devices in a mesh: wide: 64 (over z, y), narrow: 8 (over x, core).
Axes of the slice: x: 4, y: 4, z: 16, core: 2. Of those that a mesh axis runs over, the one named last changes fastest.
Arguments:
- rhs_field: float32 [512, 64, 512], P('wide', 'narrow'), may hold values from -6 to 6
- beta_cells: float32 [512, 64, 512], P('wide', 'narrow'), may hold values from 0.25 to 4
Outputs:
- solution_field: float32 [512, 64, 512], P('wide', 'narrow')
The draws below stay inside these ranges and needn't reach their ends.
All inputs are finite; a program needn't handle non-finite values.
Results may differ from the reference program's by a relative error of at most 0.0001.
Values sent between devices are 32-bit elements; how exact they have to be, the bound alone decides.
No kernel may reach another device: no remote copies, remote signals or barrier semaphores. Data moves between devices by JAX's collectives and lax.ppermute only.
A program may use at most 64 MiB of HBM per device.

```python
import math
import jax
import jax.numpy as jnp

CZ = 512
SWEEPS = 2
COARSE_SWEEPS = 8
NX = 512
NY = 64


def block_levels(key, shape, split, low, high):
    loudness, own = 1.0, jax.random.fold_in(key, 6)
    for position, blocks in split:
        draws = jnp.exp(jax.random.uniform(jax.random.fold_in(own, position), (blocks,), jnp.float32, low / len(split), high / len(split)))
        loudness = loudness * jnp.repeat(draws, shape[position] // blocks).reshape([-1 if axis == position else 1 for axis in range(len(shape))])
    return loudness


def bell_draw(stream_key, shape, deviation, reach, shards=(), dtype=jnp.bfloat16):
    values = deviation * jax.random.normal(stream_key, shape, jnp.float32)
    if shards:
        values = values * block_levels(stream_key, shape, shards, -0.22, 0.18)
    return jnp.clip(values, -reach, reach).astype(dtype)


def setup_inputs(seed: int = 0) -> dict:
    streams_of = jax.random.split(jax.random.key(seed), 3)
    rhs_field = bell_draw(streams_of[0], (NX, NY, CZ), 1.0, 6.0, ((0, 64), (1, 8)), jnp.float32)
    beta_cells = jnp.clip(jnp.exp(math.log(4.0) - 2.7725887 * jax.random.uniform(streams_of[1], (NX, NY, CZ), jnp.float32) ** block_levels(streams_of[1], (NX, NY, CZ), ((0, 64), (1, 8)), -0.2, 0.2)), 0.25, 4.0)
    return dict(rhs_field=rhs_field, beta_cells=beta_cells)


LOW_BOUND = 0.25
HIGH_BOUND = 2.0


def face_terms(padded, scale):
    face_x = scale * 0.5 * (padded[:-1, 1:-1, 1:-1] + padded[1:, 1:-1, 1:-1])
    face_y = scale * 0.5 * (padded[1:-1, :-1, 1:-1] + padded[1:-1, 1:, 1:-1])
    face_z = scale * 0.5 * (padded[1:-1, 1:-1, :-1] + padded[1:-1, 1:-1, 1:])
    diagonal = face_x[1:] + face_x[:-1] + face_y[:, 1:] + face_y[:, :-1] + face_z[:, :, 1:] + face_z[:, :, :-1]
    return (face_x, face_y, face_z, diagonal)


def apply_operator(padded, faces):
    face_x, face_y, face_z, diagonal = faces
    center = padded[1:-1, 1:-1, 1:-1]
    result = diagonal * center
    result = result - face_x[1:] * padded[2:, 1:-1, 1:-1] - face_x[:-1] * padded[:-2, 1:-1, 1:-1]
    result = result - face_y[:, 1:] * padded[1:-1, 2:, 1:-1] - face_y[:, :-1] * padded[1:-1, :-2, 1:-1]
    result = result - face_z[:, :, 1:] * padded[1:-1, 1:-1, 2:] - face_z[:, :, :-1] * padded[1:-1, 1:-1, :-2]
    return result


def chebyshev(source, start, sweeps, pad_fn, faces, from_zero):
    center_value = 0.5 * (HIGH_BOUND + LOW_BOUND)
    half_width = 0.5 * (HIGH_BOUND - LOW_BOUND)
    sigma_value = center_value / half_width
    rho_now = 1.0 / sigma_value
    iterate = start
    direction = start
    for sweep_index in range(sweeps):
        if sweep_index == 0 and from_zero:
            defect = source
        else:
            defect = source - apply_operator(pad_fn(iterate), faces)
        scaled = defect / faces[3]
        if sweep_index == 0:
            direction = scaled / center_value
        else:
            rho_next = 1.0 / (2.0 * sigma_value - rho_now)
            direction = (rho_next * rho_now) * direction + (2.0 * rho_next / half_width) * scaled
            rho_now = rho_next
        iterate = iterate + direction
    return iterate


def conjugate(source, iterations, pad_fn, faces):
    iterate = jnp.zeros_like(source)
    remainder = source
    direction = source
    norm_now = jnp.sum(remainder * remainder)
    for step_index in range(iterations):
        image = apply_operator(pad_fn(direction), faces)
        alpha = norm_now / jnp.sum(direction * image)
        iterate = iterate + alpha * direction
        remainder = remainder - alpha * image
        norm_next = jnp.sum(remainder * remainder)
        direction = remainder + (norm_next / norm_now) * direction
        norm_now = norm_next
    return iterate


def restrict(values):
    first, second, third = values.shape
    return values.reshape(first // 2, 2, second // 2, 2, third // 2, 2).mean(axis=(1, 3, 5))


def prolong(values):
    return jnp.repeat(jnp.repeat(jnp.repeat(values, 2, axis=0), 2, axis=1), 2, axis=2)


def pad_global(values):
    return jnp.pad(values, 1)


def reference(rhs_field, beta_cells):
    sources = []
    iterates = []
    level_faces = []
    source = rhs_field
    cells = beta_cells
    for level in range(3):
        faces = face_terms(pad_global(cells), 0.25 ** level)
        iterate = chebyshev(source, jnp.zeros_like(source), SWEEPS, pad_global, faces, True)
        residual = source - apply_operator(pad_global(iterate), faces)
        sources.append(source)
        iterates.append(iterate)
        level_faces.append(faces)
        source = restrict(residual)
        cells = restrict(cells)
    coarse_faces = face_terms(pad_global(cells), 0.25 ** 3)
    lower = conjugate(source, COARSE_SWEEPS, pad_global, coarse_faces)
    for level in (2, 1, 0):
        start = iterates[level] + prolong(lower)
        lower = chebyshev(sources[level], start, SWEEPS, pad_global, level_faces[level], False)
    return lower
```

```python
import functools

import jax
import jax.numpy as jnp
from jax import lax
from jax.experimental import pallas as pl
from jax.experimental.pallas import tpu as pltpu
from jax.sharding import Mesh, PartitionSpec as P

F32 = jnp.float32
BF16 = jnp.bfloat16

THETA = 0.5 * (2.0 + 0.25)
DELTA = 0.5 * (2.0 - 0.25)
SIGMA = THETA / DELTA
RHO_0 = 1.0 / SIGMA
RHO_1 = 1.0 / (2.0 * SIGMA - RHO_0)
KEEP = RHO_1 * RHO_0
GAIN = 2.0 * RHO_1 / DELTA
COARSE_SWEEPS = 8


def dot_exact(values, chooser):
    high = values.astype(BF16)
    rest = values - high.astype(F32)
    middle = rest.astype(BF16)
    low = (rest - middle.astype(F32)).astype(BF16)
    out = jnp.dot(high, chooser, preferred_element_type=F32)
    out = out + jnp.dot(middle, chooser, preferred_element_type=F32)
    return out + jnp.dot(low, chooser, preferred_element_type=F32)


def chosen_dot(chooser, values):
    high = values.astype(BF16)
    rest = values - high.astype(F32)
    middle = rest.astype(BF16)
    low = (rest - middle.astype(F32)).astype(BF16)
    out = jnp.dot(chooser, high, preferred_element_type=F32)
    out = out + jnp.dot(chooser, middle, preferred_element_type=F32)
    return out + jnp.dot(chooser, low, preferred_element_type=F32)


def iota(shape, dim):
    return lax.broadcasted_iota(jnp.int32, shape, dim)


def ones_where(mask, value=1.0):
    return jnp.where(mask, value, 0.0).astype(BF16)


def shift(values, step, axis):
    size = values.shape[axis]
    return pltpu.roll(values, (-step) % size, axis)


def plane_faces(c, c_next, fx_before, scale, axis, last, first, last_b=None, first_b=None):
    count, other = len(c), 1 - axis
    fx = [scale * (c[q] + c_next[q]) for q in range(count)]
    after = [c[q + 1] if q + 1 < count else jnp.where(last, 0.0, shift(c[0], 1, axis)) for q in range(count)]
    fa = [scale * (c[q] + after[q]) for q in range(count)]
    lowest = jnp.where(first, scale * c[0], shift(fa[-1], -1, axis))
    fb, diagonal = [], []
    for q in range(count):
        beside = shift(c[q], 1, other)
        if last_b is not None:
            beside = jnp.where(last_b, 0.0, beside)
        face = scale * (c[q] + beside)
        face_before = shift(face, -1, other)
        if first_b is not None:
            face_before = jnp.where(first_b, scale * c[q], face_before)
        diagonal.append(fx[q] + fx_before[q] + face + face_before + fa[q] + (fa[q - 1] if q else lowest))
        fb.append(face if last_b is None else jnp.where(last_b, 0.0, face))
    fa[-1] = jnp.where(last, 0.0, fa[-1])
    return fx, fa, fb, diagonal


def neighbours(u, fx, fa, fb, p, count, axis):
    other = 1 - axis
    here = [u[p, q] for q in range(count)]
    faces = [fa[p, q] for q in range(count)]
    out = []
    for q in range(count):
        face = fb[p, q]
        total = fx[p, q] * u[p + 1, q] + fx[p - 1, q] * u[p - 1, q]
        total = total + face * shift(here[q], 1, other) + shift(face * here[q], -1, other)
        if q + 1 < count:
            total = total + faces[q] * here[q + 1]
        else:
            total = total + faces[q] * shift(here[0], 1, axis)
        if q > 0:
            total = total + faces[q - 1] * here[q - 1]
        else:
            total = total + shift(faces[-1] * here[-1], -1, axis)
        out.append(total)
    return out


def loop(low, high, body):
    def step(i, carry):
        body(i)
        return carry

    lax.fori_loop(low, high, step, 0)


def inverse(c, diagonal):
    return jnp.where(c > 0.0, 1.0 / diagonal, 0.0)


C_LOW, B_LOW = 7, 6
C_PLANES, B_PLANES = 8 + 2 * C_LOW, 8 + 2 * B_LOW
SENT = C_LOW + B_LOW
WIDE_PLANES = C_PLANES + B_PLANES


def split_kernel(rhs, beta, own, up, down):
    z = iota((512, 512), 0)
    k = iota((512, 512), 1)
    chooser = ones_where(z == 4 * (k % 128) + k // 128)
    for field, source in enumerate((beta, rhs)):
        out = dot_exact(source[...].reshape(64, 512), chooser)
        for x in range(8):
            for q in range(4):
                tile = out[8 * x : 8 * x + 8, 128 * q : 128 * q + 128]
                own[8 * field + x, q] = tile
                width = (C_LOW, B_LOW)[field]
                start = (0, C_LOW)[field]
                if x >= 8 - width:
                    up[start + x - (8 - width), q] = tile
                if x < width:
                    down[start + x, q] = tile


def widen_kernel(own, below, above, out, *, wide):
    index = lax.axis_index("z") * lax.axis_size("y") + lax.axis_index("y")
    keep_low = jnp.where(index > 0, 1.0, 0.0).astype(F32)
    keep_high = jnp.where(index < wide - 1, 1.0, 0.0).astype(F32)
    for j in range(C_LOW):
        out[j] = below[j] * keep_low
        out[C_LOW + 8 + j] = above[j] * keep_high
    for j in range(8):
        out[C_LOW + j] = own[j]
        out[C_PLANES + B_LOW + j] = own[8 + j]
    for j in range(B_LOW):
        out[C_PLANES + j] = below[C_LOW + j]
        out[C_PLANES + B_LOW + 8 + j] = above[C_LOW + j]


def down_kernel(mid, left, right, packed, x0, b0, fx, fy, fz, dinv, c1, b1, fx1, fy1, fz1, dinv1, diag, first, sums, diag1, first1, x1, *, group):
    n = lax.axis_index("n")
    keep_left = jnp.where(n > 0, 1.0, 0.0).astype(F32)
    keep_right = jnp.where(n < lax.axis_size("n") - 1, 1.0, 0.0).astype(F32)
    lane = iota((24, 128), 1)
    last, begin = lane == 127, lane == 0

    def cells(p):
        j = p - 1
        return [jnp.concatenate([left[j, q] * keep_left, mid[j, q], right[j, q] * keep_right], axis=0) for q in range(4)]

    def source(p):
        j = p - 2 + C_PLANES
        return [jnp.concatenate([left[j, q], mid[j, q], right[j, q]], axis=0) for q in range(4)]

    before, after = cells(1), cells(2)
    for q in range(4):
        fx[1, q] = 0.5 * (before[q] + after[q])

    def faces_0(p):
        c, c_next, b = cells(p), cells(p + 1), source(p)
        gx, gz, gy, d = plane_faces(c, c_next, [fx[p - 1, q] for q in range(4)], 0.5, 1, last, begin)
        for q in range(4):
            fx[p, q], fy[p, q], fz[p, q], diag[p, q] = gx[q], gy[q], gz[q], d[q]
            inv = inverse(c[q], d[q])
            dinv[p, q] = inv
            b0[p, q] = b[q]
            first[p, q] = b[q] * inv * (1.0 / THETA)

    loop(2, 22, faces_0)

    def second_0(p):
        near = neighbours(first, fx, fz, fy, p, 4, 1)
        for q in range(4):
            x0[p, q] = (1.0 + KEEP - GAIN) * first[p, q] + GAIN * (b0[p, q] + near[q]) * dinv[p, q]

    loop(3, 21, second_0)

    def residual_0(k):
        total = [jnp.zeros((24, 128), F32)] * 2
        for p in (4 + 2 * k, 5 + 2 * k):
            near = neighbours(x0, fx, fz, fy, p, 4, 1)
            for q in range(4):
                total[q // 2] = total[q // 2] + (b0[p, q] + near[q] - diag[p, q] * x0[p, q])
        for q in range(2):
            sums[k, q, 0:24] = total[q]
            sums[k, q, 24:32] = jnp.zeros((8, 128), F32)

    loop(0, 8, residual_0)

    def cells_1(k):
        one, two = cells(2 + 2 * k), cells(3 + 2 * k)
        for q in range(2):
            sums[8 + k, q, 0:24] = (one[2 * q] + one[2 * q + 1]) + (two[2 * q] + two[2 * q + 1])
            sums[8 + k, q, 24:32] = jnp.zeros((8, 128), F32)

    loop(0, 10, cells_1)

    def halve(k, q):
        return 0.125 * (sums[k, q, pl.ds(0, 16, stride=2), :] + sums[k, q, pl.ds(1, 16, stride=2), :])

    for q in range(2):
        loop(0, 8, lambda k, q=q: b1.__setitem__((k + 1, q), halve(k, q)))
        loop(0, 10, lambda k, q=q: c1.__setitem__((k, q), halve(8 + k, q)))

    lane = iota((16, 128), 1)
    last_1, begin_1 = lane == 127, lane == 0
    for q in range(2):
        fx1[0, q] = 0.125 * (c1[0, q] + c1[1, q])

    def faces_1(p):
        c, c_next = [c1[p, q] for q in range(2)], [c1[p + 1, q] for q in range(2)]
        gx, gz, gy, d = plane_faces(c, c_next, [fx1[p - 1, q] for q in range(2)], 0.125, 1, last_1, begin_1)
        for q in range(2):
            fx1[p, q], fy1[p, q], fz1[p, q], diag1[p, q] = gx[q], gy[q], gz[q], d[q]
            inv = inverse(c[q], d[q])
            dinv1[p, q] = inv
            first1[p, q] = b1[p, q] * inv * (1.0 / THETA)

    loop(1, 9, faces_1)

    def second_1(p):
        near = neighbours(first1, fx1, fz1, fy1, p, 2, 1)
        for q in range(2):
            x1[p, q] = (1.0 + KEEP - GAIN) * first1[p, q] + GAIN * (b1[p, q] + near[q]) * dinv1[p, q]

    loop(2, 8, second_1)

    for x in range(4):
        for q in range(2):
            packed[0, x, 4 * q : 4 * q + 4] = x1[3 + x, q, 4:8]
    for x in range(2):
        total = jnp.zeros((16, 128), F32)
        cell = jnp.zeros((16, 128), F32)
        for p in (3 + 2 * x, 4 + 2 * x):
            near = neighbours(x1, fx1, fz1, fy1, p, 2, 1)
            for q in range(2):
                total = total + (b1[p, q] + near[q] - diag1[p, q] * x1[p, q])
                cell = cell + c1[p, q]
        total = 0.125 * (total + shift(total, 1, 0))
        cell = 0.125 * (cell + shift(cell, 1, 0))
        for yy in range(2):
            packed[0, 4, 2 * x + yy : 2 * x + yy + 1] = total[4 + 2 * yy : 5 + 2 * yy]
            packed[0, 4, 4 + 2 * x + yy : 5 + 2 * x + yy] = cell[4 + 2 * yy : 5 + 2 * yy]

    def copy(s):
        packed[s] = packed[0]

    loop(1, group, copy)


def edge_kernel(plane, up, down, *, depth):
    n = lax.axis_index("n")
    size = lax.axis_size("n")

    def slab(s):
        tile = plane[s, 4]
        up[s] = tile
        down[s] = tile

    loop(0, depth * size, slab)
    for k in range(3):
        place = jnp.clip(n + (k - 1), 0, size - 1)
        for x in range(4):
            up[depth * size + 4 * k + x] = plane[(depth - 1) * size + place, x]
            down[depth * size + 4 * k + x] = plane[place, x]


def middle_kernel(plane, below, above, sent, x2, b2, fx, fy, fz, dinv, x1, c2, diag, first, *, depth, tall):
    z, y, n = lax.axis_index("z"), lax.axis_index("y"), lax.axis_index("n")
    size = lax.axis_size("n")
    keep_low = jnp.where(z > 0, 1.0, 0.0).astype(F32)
    keep_high = jnp.where(z < tall - 1, 1.0, 0.0).astype(F32)
    width = 2 * depth
    for yb in range(depth):
        for x in range(2):
            for yy in range(2):
                r = 2 * x + yy
                place = 2 * yb + x
                own = yb * size * 40 + 32 + r
                edge = yb * size * 8 + r
                b2[place, yy] = below[pl.ds(edge, 8, stride=8), :]
                b2[width + place, yy] = plane[pl.ds(own, 8, stride=40), :]
                b2[2 * width + place, yy] = above[pl.ds(edge, 8, stride=8), :]
                c2[place, yy] = below[pl.ds(edge + 4, 8, stride=8), :] * keep_low
                c2[width + place, yy] = plane[pl.ds(own + 4, 8, stride=40), :]
                c2[2 * width + place, yy] = above[pl.ds(edge + 4, 8, stride=8), :] * keep_high

    scale = 0.5 / 16.0
    shape = (8, 128)
    row, lane = iota(shape, 0), iota(shape, 1)
    last, begin, last_b, begin_b = row == 7, row == 0, lane == 127, lane == 0
    for q in range(2):
        fx[0, q] = scale * (c2[0, q] + c2[1, q])

    def faces_2(p):
        c, c_next = [c2[p, q] for q in range(2)], [c2[p + 1, q] for q in range(2)]
        gx, gy, gz, d = plane_faces(c, c_next, [fx[p - 1, q] for q in range(2)], scale, 0, last, begin, last_b, begin_b)
        for q in range(2):
            fx[p, q], fy[p, q], fz[p, q], diag[p, q] = gx[q], gy[q], gz[q], d[q]
            inv = inverse(c[q], d[q])
            dinv[p, q] = inv
            first[p, q] = b2[p, q] * inv * (1.0 / THETA)

    loop(1, 3 * width - 1, faces_2)

    def second_2(p):
        near = neighbours(first, fx, fy, fz, p, 2, 0)
        for q in range(2):
            x2[p, q] = (1.0 + KEEP - GAIN) * first[p, q] + GAIN * (b2[p, q] + near[q]) * dinv[p, q]

    loop(2, 3 * width - 2, second_2)

    totals, cell_sums = [], []
    for j in range(depth):
        total = jnp.zeros(shape, F32)
        cell = jnp.zeros(shape, F32)
        for p in (width + 2 * j, width + 2 * j + 1):
            near = neighbours(x2, fx, fy, fz, p, 2, 0)
            for q in range(2):
                total = total + (b2[p, q] + near[q] - diag[p, q] * x2[p, q])
                cell = cell + c2[p, q]
        totals.append(total)
        cell_sums.append(cell)
    zz, k = iota((128, 128), 0), iota((128, 128), 1)
    low_half = ones_where(k == zz // 2, 0.125)
    high_half = ones_where(k == zz // 2 + 64, 0.125)
    coarse = dot_exact(jnp.concatenate(totals, axis=0), low_half) + dot_exact(jnp.concatenate(cell_sums, axis=0), high_half)
    coarse = coarse.reshape(depth, 8, 128)
    for s in range(tall):
        sent[s] = coarse

    for x in range(4):
        for k in range(3):
            place = jnp.clip(n + (k - 1), 0, size - 1)

            def block(yb):
                start = pl.multiple_of((yb * size + place) * 40 + 8 * x, 8)
                return plane[pl.ds(start, 8), :]

            edge = 8 * (depth * size + 4 * k + x)
            tiles = {
                -1: jnp.where(y == 0, below[edge : edge + 8], block(jnp.maximum(y - 1, 0))),
                0: block(y),
                1: jnp.where(y == depth - 1, above[edge : edge + 8], block(jnp.minimum(y + 1, depth - 1))),
            }
            for dx, tile in tiles.items():
                p = 3 + 4 * dx + x
                if 0 <= p < 10:
                    for q in range(2):
                        x1[p, q, 4 * k : 4 * k + 4] = tile[4 * q : 4 * q + 4]
    for p in range(10):
        for q in range(2):
            x1[p, q, 12:16] = jnp.zeros((4, 128), F32)


def sweeps(start, mid, out, source, fx, fa, fb, dinv, low, high, count, axis):
    def one(p):
        near = neighbours(start, fx, fa, fb, p, count, axis)
        for q in range(count):
            mid[p, q] = (1.0 - 1.0 / THETA) * start[p, q] + (1.0 / THETA) * ((source[p, q] + near[q]) * dinv[p, q])

    loop(low - 1, high + 1, one)

    def two(p):
        near = neighbours(mid, fx, fa, fb, p, count, axis)
        for q in range(count):
            value = (1.0 - GAIN + KEEP) * mid[p, q] - KEEP * start[p, q]
            out(p, q, value + GAIN * ((source[p, q] + near[q]) * dinv[p, q]))

    loop(low, high, two)


def up_kernel(gathered, x1h, x2, b2, fx2, fy2, fz2, dinv2, c1, b1, fx1, fy1, fz1, dinv1, x0, b0, fx, fy, fz, dinv, result,
              c3, p3, r3, x3, i3, fx3, fy3, fz3, d3, s2, m2, f2, s1, m1, f1, s0, m0, f0, *, depth, tall):
    z, y, n = lax.axis_index("z"), lax.axis_index("y"), lax.axis_index("n")
    half = depth * tall // 2
    shape = (8, 128)
    row, lane = iota(shape, 0), iota(shape, 1)
    upper = lane >= 64

    def unpack(i):
        one, two = gathered[i], gathered[i + half]
        b = jnp.where(upper, pltpu.roll(two, 64, 1), one)
        c3[i + 1, 0] = jnp.where(upper, two, pltpu.roll(one, 64, 1))
        r3[i + 1, 0] = b
        p3[i + 1, 0] = b
        x3[i + 1, 0] = jnp.zeros(shape, F32)

    loop(0, half, unpack)

    def wrap(ref):
        ref[0, 0] = jnp.where(upper, pltpu.roll(ref[half, 0], 64, 1), 0.0)
        ref[half + 1, 0] = jnp.where(upper, 0.0, pltpu.roll(ref[1, 0], 64, 1))

    wrap(c3)
    scale = 0.5 / 64.0
    fx3[0, 0] = scale * (c3[0, 0] + c3[1, 0])

    def faces_3(p):
        gx, gy, gz, d = plane_faces([c3[p, 0]], [c3[p + 1, 0]], [fx3[p - 1, 0]], scale, 0, row == 7, row == 0, lane % 64 == 63, lane % 64 == 0)
        fx3[p, 0], fy3[p, 0], fz3[p, 0], d3[p, 0] = gx[0], gy[0], gz[0], d[0]

    loop(1, half + 1, faces_3)

    def whole(parts):
        total = functools.reduce(lambda a, b: a + b, parts)
        return jnp.sum(jnp.sum(total, axis=0, keepdims=True), axis=1, keepdims=True)

    def spread(values):
        parts = [jnp.zeros(shape, F32)] * 4
        for i, value in enumerate(values):
            parts[i % 4] = parts[i % 4] + value
        return whole(parts)

    start_norm = spread([r3[i + 1, 0] * r3[i + 1, 0] for i in range(half)])

    def iterate(_, norm):
        wrap(p3)
        products = []
        for p in range(1, half + 1):
            here = p3[p, 0]
            image = d3[p, 0] * here - neighbours(p3, fx3, fy3, fz3, p, 1, 0)[0]
            i3[p, 0] = image
            products.append(here * image)
        alpha = norm / spread(products)
        squares = []
        for p in range(1, half + 1):
            x3[p, 0] = x3[p, 0] + alpha * p3[p, 0]
            rest = r3[p, 0] - alpha * i3[p, 0]
            r3[p, 0] = rest
            squares.append(rest * rest)
        new = spread(squares)
        beta = new / norm
        for p in range(1, half + 1):
            p3[p, 0] = r3[p, 0] + beta * p3[p, 0]
        return new

    lax.fori_loop(0, COARSE_SWEEPS, iterate, start_norm)

    base = 2 * depth + 2 * y - 4
    tiles = []
    for j in range(5):
        place = jnp.clip(depth * z + y - 2 + j, 0, 2 * half - 1)
        high = place >= half
        tile = x3[jnp.where(high, place - half, place) + 1, 0]
        tiles.append(jnp.where(high, pltpu.roll(tile, 64, 1), tile))
    k, zz = iota((128, 128), 0), iota((128, 128), 1)
    fine = dot_exact(jnp.concatenate(tiles, axis=0), ones_where(k == zz // 2))
    for j in range(5):
        add = fine[8 * j : 8 * j + 8]
        for p in (base + 2 * j, base + 2 * j + 1):
            for q in range(2):
                s2[p, q] = jnp.where(dinv2[p, q] > 0.0, x2[p, q] + add, 0.0)

    def keep_2(p, q, value):
        f2[p, q] = value

    sweeps(s2, m2, keep_2, b2, fx2, fy2, fz2, dinv2, base + 2, base + 8, 2, 0)

    wide = jnp.concatenate([jnp.concatenate([f2[base + 2 + k, 0], f2[base + 2 + k, 1]], axis=0) for k in range(6)], axis=1)
    r, k = iota((16, 16), 0), iota((16, 16), 1)
    from_n = n + r // 4 - 1
    pick = ones_where((k == (r // 2) % 2 * 8 + from_n) & (from_n >= 0) & (from_n < 8))
    fine = chosen_dot(pick, wide)
    for p in range(10):
        k = (p + 1) // 2
        for q in range(2):
            s1[p, q] = jnp.where(c1[p, q] > 0.0, x1h[p, q] + fine[:, 128 * k : 128 * k + 128], 0.0)

    def keep_1(p, q, value):
        f1[p, q] = value

    sweeps(s1, m1, keep_1, b1, fx1, fz1, fy1, dinv1, 2, 8, 2, 1)

    wide = jnp.concatenate([f1[p, q] for p in range(2, 8) for q in range(2)], axis=1)
    r, k = iota((24, 16), 0), iota((24, 16), 1)
    fine = chosen_dot(ones_where(k == r // 2), wide)
    for p in range(6, 18):
        for q in range(4):
            j = 2 * (p // 2 - 3) + q // 2
            s0[p, q] = jnp.where(dinv[p, q] > 0.0, x0[p, q] + fine[:, 128 * j : 128 * j + 128], 0.0)

    def keep_0(p, q, value):
        start = (p - 8) * 8
        if not isinstance(start, int):
            start = pl.multiple_of(start, 8)
        f0[pl.ds(start, 8), 128 * q : 128 * q + 128] = value[8:16]

    sweeps(s0, m0, keep_0, b0, fx, fz, fy, dinv, 8, 16, 4, 1)
    k, z0 = iota((512, 512), 0), iota((512, 512), 1)
    back = ones_where(z0 == 4 * (k % 128) + k // 128)
    result[...] = dot_exact(f0[...], back).reshape(8, 8, 512)


def call(kernel, outs, *operands, scratch=(), limit=40):
    shapes = [jax.ShapeDtypeStruct(shape, F32) for shape in outs]
    return pl.pallas_call(
        kernel,
        out_shape=shapes,
        in_specs=[pl.BlockSpec(memory_space=pltpu.VMEM)] * len(operands),
        out_specs=[pl.BlockSpec(memory_space=pltpu.VMEM)] * len(outs),
        scratch_shapes=[pltpu.VMEM(shape, F32) for shape in scratch],
        compiler_params=pltpu.CompilerParams(vmem_limit_bytes=limit * 2**20),
    )(*operands)


def ring(axis_size, step):
    return [(i, (i + step) % axis_size) for i in range(axis_size)]


def shards(rhs_field, beta_cells):
    tall, depth, size = lax.axis_size("z"), lax.axis_size("y"), lax.axis_size("n")
    wide, group = tall * depth, depth * size
    own, up, down = call(
        split_kernel, [(16, 4, 8, 128), (SENT, 4, 8, 128), (SENT, 4, 8, 128)], rhs_field, beta_cells
    )
    below = lax.ppermute(up, ("z", "y"), ring(wide, 1))
    above = lax.ppermute(down, ("z", "y"), ring(wide, -1))
    (mid,) = call(functools.partial(widen_kernel, wide=wide), [(WIDE_PLANES, 4, 8, 128)], own, below, above)
    left = lax.ppermute(mid, "n", ring(size, 1))
    right = lax.ppermute(mid, "n", ring(size, -1))
    fine, coarse = (24, 4, 24, 128), (10, 2, 16, 128)
    outs = call(
        functools.partial(down_kernel, group=group),
        [(group, 5, 8, 128)] + [fine] * 6 + [coarse] * 6,
        mid, left, right,
        scratch=[fine, fine, (18, 2, 32, 128), coarse, coarse, coarse],
    )
    packed, level_zero, level_one = outs[0], outs[1:7], outs[7:13]
    plane = lax.all_to_all(packed, ("y", "n"), 0, 0)
    edge = group + 12
    up, down = call(functools.partial(edge_kernel, depth=depth), [(edge, 8, 128)] * 2, plane)
    below = lax.ppermute(up, "z", ring(tall, 1))
    above = lax.ppermute(down, "z", ring(tall, -1))
    slab = (6 * depth, 2, 8, 128)
    outs = call(
        functools.partial(middle_kernel, depth=depth, tall=tall),
        [(tall, depth, 8, 128)] + [slab] * 6 + [coarse],
        plane.reshape(group * 40, 128), below.reshape(edge * 8, 128), above.reshape(edge * 8, 128),
        scratch=[slab, slab, slab],
    )
    sent, level_two, x1h = outs[0], outs[1:7], outs[7]
    gathered = lax.all_to_all(sent, "z", 0, 0)
    packed_3 = (wide // 2 + 2, 1, 8, 128)
    (result,) = call(
        functools.partial(up_kernel, depth=depth, tall=tall),
        [(8, 8, 512)],
        gathered.reshape(wide, 8, 128), x1h, *level_two, *level_one, *level_zero,
        scratch=[packed_3] * 9 + [slab] * 3 + [coarse] * 3 + [fine] * 2 + [(64, 512)],
    )
    return result


def solution(mesh):
    wide, size = mesh.shape["wide"], mesh.shape["narrow"]
    inner = Mesh(mesh.devices.reshape(wide // 4, 4, size), ("z", "y", "n"))
    spec = P(("z", "y"), "n", None)
    return jax.shard_map(shards, mesh=inner, in_specs=(spec, spec), out_specs=spec, check_vma=False)
```

```python
import functools

import jax
import jax.numpy as jnp
from jax import lax
from jax.experimental import pallas as pl
from jax.experimental.pallas import tpu as pltpu
from jax.sharding import Mesh, PartitionSpec as P

F32 = jnp.float32
BF16 = jnp.bfloat16

THETA = 0.5 * (2.0 + 0.25)
DELTA = 0.5 * (2.0 - 0.25)
SIGMA = THETA / DELTA
RHO_0 = 1.0 / SIGMA
RHO_1 = 1.0 / (2.0 * SIGMA - RHO_0)
KEEP = RHO_1 * RHO_0
GAIN = 2.0 * RHO_1 / DELTA
COARSE_SWEEPS = 8


def dot_exact(values, chooser):
    high = values.astype(BF16)
    rest = values - high.astype(F32)
    middle = rest.astype(BF16)
    low = (rest - middle.astype(F32)).astype(BF16)
    out = jnp.dot(high, chooser, preferred_element_type=F32)
    out = out + jnp.dot(middle, chooser, preferred_element_type=F32)
    return out + jnp.dot(low, chooser, preferred_element_type=F32)


def chosen_dot(chooser, values):
    high = values.astype(BF16)
    rest = values - high.astype(F32)
    middle = rest.astype(BF16)
    low = (rest - middle.astype(F32)).astype(BF16)
    out = jnp.dot(chooser, high, preferred_element_type=F32)
    out = out + jnp.dot(chooser, middle, preferred_element_type=F32)
    return out + jnp.dot(chooser, low, preferred_element_type=F32)


def iota(shape, dim):
    return lax.broadcasted_iota(jnp.int32, shape, dim)


def ones_where(mask, value=1.0):
    return jnp.where(mask, value, 0.0).astype(BF16)


def shift(values, step, axis):
    size = values.shape[axis]
    return pltpu.roll(values, (-step) % size, axis)


def plane_faces(c, c_next, fx_before, scale, axis, last, first, last_b=None, first_b=None):
    count, other = len(c), 1 - axis
    fx = [scale * (c[q] + c_next[q]) for q in range(count)]
    after = [c[q + 1] if q + 1 < count else jnp.where(last, 0.0, shift(c[0], 1, axis)) for q in range(count)]
    fa = [scale * (c[q] + after[q]) for q in range(count)]
    lowest = jnp.where(first, scale * c[0], shift(fa[-1], -1, axis))
    fb, diagonal = [], []
    for q in range(count):
        beside = shift(c[q], 1, other)
        if last_b is not None:
            beside = jnp.where(last_b, 0.0, beside)
        face = scale * (c[q] + beside)
        face_before = shift(face, -1, other)
        if first_b is not None:
            face_before = jnp.where(first_b, scale * c[q], face_before)
        diagonal.append(fx[q] + fx_before[q] + face + face_before + fa[q] + (fa[q - 1] if q else lowest))
        fb.append(face if last_b is None else jnp.where(last_b, 0.0, face))
    fa[-1] = jnp.where(last, 0.0, fa[-1])
    return fx, fa, fb, diagonal


def neighbours(u, fx, fa, fb, p, count, axis):
    other = 1 - axis
    here = [u[p, q] for q in range(count)]
    faces = [fa[p, q] for q in range(count)]
    out = []
    for q in range(count):
        face = fb[p, q]
        total = fx[p, q] * u[p + 1, q] + fx[p - 1, q] * u[p - 1, q]
        total = total + face * shift(here[q], 1, other) + shift(face * here[q], -1, other)
        if q + 1 < count:
            total = total + faces[q] * here[q + 1]
        else:
            total = total + faces[q] * shift(here[0], 1, axis)
        if q > 0:
            total = total + faces[q - 1] * here[q - 1]
        else:
            total = total + shift(faces[-1] * here[-1], -1, axis)
        out.append(total)
    return out


def loop(low, high, body):
    for k in range(high - low):
        body(low + k)


def inverse(c, diagonal):
    return jnp.where(c > 0.0, 1.0 / diagonal, 0.0)


C_LOW, B_LOW = 7, 6
SENT = C_LOW + B_LOW

CORNERS = (
    (0, 1, 0, 0), (0, 2, 0, 0), (0, 3, 7, 2), (0, 4, 6, 3), (0, 5, 0, 0),
    (1, 1, 6, 2), (1, 2, 0, 0), (1, 3, 5, 3), (1, 4, 0, 0),
)


def split_kernel(rhs_hbm, beta_hbm, own, up, down, rhs, beta, sems):
    copies = [
        pltpu.make_async_copy(beta_hbm, beta, sems.at[0]),
        pltpu.make_async_copy(rhs_hbm, rhs, sems.at[1]),
    ]
    for copy in copies:
        copy.start()
    z = iota((512, 512), 0)
    k = iota((512, 512), 1)
    chooser = ones_where(z == 4 * (k % 128) + k // 128)
    for field, source in enumerate((beta, rhs)):
        copies[field].wait()
        out = dot_exact(source[...].reshape(64, 512), chooser)
        for x in range(8):
            for q in range(4):
                tile = out[8 * x : 8 * x + 8, 128 * q : 128 * q + 128]
                own[8 * field + x, q] = tile
                width = (C_LOW, B_LOW)[field]
                start = (0, C_LOW)[field]
                if x >= 8 - width:
                    up[start + x - (8 - width), q] = tile
                if x < width:
                    down[start + x, q] = tile


def side_index(side, field, distance):
    width, start = (C_LOW, B_LOW)[field], (0, C_LOW)[field]
    return start + (width - distance if side == 0 else distance - 1)


def corner_kernel(below, above, right, left, *, wide):
    index = lax.axis_index("z") * lax.axis_size("y") + lax.axis_index("y")
    keep = [jnp.where(index > 0, 1.0, 0.0).astype(F32), jnp.where(index < wide - 1, 1.0, 0.0).astype(F32)]
    row = iota((8, 128), 0)
    for side, planes in enumerate((below, above)):
        for t, (field, one, two, rows) in enumerate(CORNERS):
            place = side * len(CORNERS) + t
            for q in range(4):
                tile = planes[side_index(side, field, one), q]
                to_right = to_left = tile
                if two:
                    other = planes[side_index(side, field, two), q]
                    to_right = jnp.where(row >= rows, tile, pltpu.roll(other, rows, 0))
                    to_left = jnp.where(row < 8 - rows, tile, pltpu.roll(other, 8 - rows, 0))
                if field == 0:
                    to_right, to_left = to_right * keep[side], to_left * keep[side]
                right[place, q] = to_right
                left[place, q] = to_left


def down_kernel(own, below, above, own_left, own_right, corner_left, corner_right, packed, x0, b0, fx, fy, fz, dinv, c1, x1, r1, fx1, fy1, fz1, dinv1, diag, first, sums, diag1, first1, b1, parts, *, wide, depth):
    n = lax.axis_index("n")
    index = lax.axis_index("z") * lax.axis_size("y") + lax.axis_index("y")
    keep_wide = [jnp.where(index > 0, 1.0, 0.0).astype(F32), jnp.where(index < wide - 1, 1.0, 0.0).astype(F32)]
    keep_left = jnp.where(n > 0, 1.0, 0.0).astype(F32)
    keep_right = jnp.where(n < lax.axis_size("n") - 1, 1.0, 0.0).astype(F32)
    lane = iota((24, 128), 1)
    last, begin = lane == 127, lane == 0

    corner = {}
    for t, (field, one, two, rows) in enumerate(CORNERS):
        corner[field, one] = (t, 0)
        if two:
            corner[field, two] = (t, rows)

    def plane(field, p, keep_0, keep_1):
        x = p - 8
        out = []
        for q in range(4):
            if 0 <= x < 8:
                parts = [own_left[8 * field + x, q], own[8 * field + x, q], own_right[8 * field + x, q]]
            else:
                side, distance = (0, -x) if x < 0 else (1, x - 7)
                t, rows = corner[field, distance]
                place = side * len(CORNERS) + t
                parts = [corner_left[place, q], (below, above)[side][side_index(side, field, distance), q], corner_right[place, q]]
                if rows:
                    parts[0] = pltpu.roll(parts[0], 8 - rows, 0)
                    parts[2] = pltpu.roll(parts[2], rows, 0)
                if field == 0:
                    parts[1] = parts[1] * keep_wide[side]
            out.append(jnp.concatenate([parts[0] * keep_0, parts[1], parts[2] * keep_1] if field == 0 else parts, axis=0))
        return out

    def cells(p):
        return plane(0, p, keep_left, keep_right)

    def source(p):
        return plane(1, p, None, None)

    before, after = cells(1), cells(2)
    for q in range(4):
        fx[1, q] = 0.5 * (before[q] + after[q])

    def faces_0(p):
        c, c_next, b = cells(p), cells(p + 1), source(p)
        gx, gz, gy, d = plane_faces(c, c_next, [fx[p - 1, q] for q in range(4)], 0.5, 1, last, begin)
        for q in range(4):
            fx[p, q], fy[p, q], fz[p, q], diag[p, q] = gx[q], gy[q], gz[q], d[q]
            inv = inverse(c[q], d[q])
            dinv[p, q] = inv
            b0[p, q] = b[q]
            first[p, q] = b[q] * inv * (1.0 / THETA)

    loop(2, 22, faces_0)

    def second_0(p):
        near = neighbours(first, fx, fz, fy, p, 4, 1)
        for q in range(4):
            x0[p, q] = (1.0 + KEEP - GAIN) * first[p, q] + GAIN * (b0[p, q] + near[q]) * dinv[p, q]

    loop(3, 21, second_0)

    def residual_0(k):
        total = [jnp.zeros((24, 128), F32)] * 2
        for p in (4 + 2 * k, 5 + 2 * k):
            near = neighbours(x0, fx, fz, fy, p, 4, 1)
            for q in range(4):
                total[q // 2] = total[q // 2] + (b0[p, q] + near[q] - diag[p, q] * x0[p, q])
        for q in range(2):
            sums[k, q, 0:24] = total[q]
            sums[k, q, 24:32] = jnp.zeros((8, 128), F32)

    loop(0, 8, residual_0)

    def cells_1(k):
        one, two = cells(2 + 2 * k), cells(3 + 2 * k)
        for q in range(2):
            sums[8 + k, q, 0:24] = (one[2 * q] + one[2 * q + 1]) + (two[2 * q] + two[2 * q + 1])
            sums[8 + k, q, 24:32] = jnp.zeros((8, 128), F32)

    loop(0, 10, cells_1)

    def halve(k, q):
        return 0.125 * (sums[k, q, pl.ds(0, 16, stride=2), :] + sums[k, q, pl.ds(1, 16, stride=2), :])

    for q in range(2):
        loop(0, 8, lambda k, q=q: b1.__setitem__((k + 1, q), halve(k, q)))
        loop(0, 10, lambda k, q=q: c1.__setitem__((k, q), halve(8 + k, q)))

    lane = iota((16, 128), 1)
    last_1, begin_1 = lane == 127, lane == 0
    for q in range(2):
        fx1[0, q] = 0.125 * (c1[0, q] + c1[1, q])

    def faces_1(p):
        c, c_next = [c1[p, q] for q in range(2)], [c1[p + 1, q] for q in range(2)]
        gx, gz, gy, d = plane_faces(c, c_next, [fx1[p - 1, q] for q in range(2)], 0.125, 1, last_1, begin_1)
        for q in range(2):
            fx1[p, q], fy1[p, q], fz1[p, q], diag1[p, q] = gx[q], gy[q], gz[q], d[q]
            inv = inverse(c[q], d[q])
            dinv1[p, q] = inv
            first1[p, q] = b1[p, q] * inv * (1.0 / THETA)

    loop(1, 9, faces_1)

    def second_1(p):
        near = neighbours(first1, fx1, fz1, fy1, p, 2, 1)
        for q in range(2):
            x1[p, q] = (1.0 + KEEP - GAIN) * first1[p, q] + GAIN * (b1[p, q] + near[q]) * dinv1[p, q]

    loop(2, 8, second_1)

    y, size = lax.axis_index("y"), lax.axis_size("n")
    for x in range(2):
        total = jnp.zeros((16, 128), F32)
        cell = jnp.zeros((16, 128), F32)
        for p in (3 + 2 * x, 4 + 2 * x):
            near = neighbours(x1, fx1, fz1, fy1, p, 2, 1)
            for q in range(2):
                rest = b1[p, q] + near[q] - diag1[p, q] * x1[p, q]
                r1[p, q] = rest
                total = total + rest
                cell = cell + c1[p, q]
                place = p - 3
                parts[place // 2, place % 2, 4 * q : 4 * q + 4] = rest[4:8]
                row = 4 * (place % 2) + 2 * q
                parts[2, place // 2, row : row + 2] = rest[6:8]
                parts[3, place // 2, row : row + 2] = rest[4:6]
        total = 0.125 * (total + shift(total, 1, 0))
        cell = 0.125 * (cell + shift(cell, 1, 0))
        for yy in range(2):
            packed[0, 2, 2 * x + yy : 2 * x + yy + 1] = total[4 + 2 * yy : 5 + 2 * yy]
            packed[0, 2, 4 + 2 * x + yy : 5 + 2 * x + yy] = cell[4 + 2 * yy : 5 + 2 * yy]

    level_two = packed[0, 2]
    for y_to in range(depth):
        ahead = (y_to - y + depth) % depth
        for n_to in range(size):
            beside = jnp.where(n_to > n, 2, 3)
            part = jnp.where(ahead == 0, beside, jnp.where(ahead == 1, 1, 0))
            s = y_to * size + n_to
            packed[s, 0] = parts[part, 0]
            packed[s, 1] = parts[part, 1]
            packed[s, 2] = level_two


def edge_kernel(plane, up, down, *, depth):
    n = lax.axis_index("n")
    size = lax.axis_size("n")

    count = (depth - 1) * size
    for s in range(count):
        up[s] = plane[size + s, 2]
        down[s] = plane[s, 2]
    for k in range(3):
        place = jnp.clip(n + (k - 1), 0, size - 1)
        for j in range(2):
            up[count + 2 * k + j] = plane[count + place, j]
            down[count + 2 * k + j] = plane[place, j]


def middle_kernel(plane, below, above, r1, sent, x2, r2, fx, fy, fz, dinv, r1h, b2, c2, diag, first, *, depth, tall):
    z, y, n = lax.axis_index("z"), lax.axis_index("y"), lax.axis_index("n")
    size = lax.axis_size("n")
    keep_low = jnp.where(z > 0, 1.0, 0.0).astype(F32)
    keep_high = jnp.where(z < tall - 1, 1.0, 0.0).astype(F32)
    width = 2 * depth
    for yb in range(depth):
        for x in range(2):
            for yy in range(2):
                r = 2 * x + yy
                place = 2 * yb + x
                own = yb * size * 24 + 16 + r
                b2[width + place, yy] = plane[pl.ds(own, 8, stride=24), :]
                c2[width + place, yy] = plane[pl.ds(own + 4, 8, stride=24), :]
                if yb > 0:
                    edge = (yb - 1) * size * 8 + r
                    b2[place, yy] = below[pl.ds(edge, 8, stride=8), :]
                    c2[place, yy] = below[pl.ds(edge + 4, 8, stride=8), :] * keep_low
                if yb < depth - 1:
                    edge = yb * size * 8 + r
                    b2[2 * width + place, yy] = above[pl.ds(edge, 8, stride=8), :]
                    c2[2 * width + place, yy] = above[pl.ds(edge + 4, 8, stride=8), :] * keep_high

    scale = 0.5 / 16.0
    shape = (8, 128)
    row, lane = iota(shape, 0), iota(shape, 1)
    last, begin, last_b, begin_b = row == 7, row == 0, lane == 127, lane == 0
    for q in range(2):
        fx[2, q] = scale * (c2[2, q] + c2[3, q])

    def faces_2(p):
        c, c_next = [c2[p, q] for q in range(2)], [c2[p + 1, q] for q in range(2)]
        gx, gy, gz, d = plane_faces(c, c_next, [fx[p - 1, q] for q in range(2)], scale, 0, last, begin, last_b, begin_b)
        for q in range(2):
            fx[p, q], fy[p, q], fz[p, q], diag[p, q] = gx[q], gy[q], gz[q], d[q]
            inv = inverse(c[q], d[q])
            dinv[p, q] = inv
            first[p, q] = b2[p, q] * inv * (1.0 / THETA)

    loop(3, 3 * width - 3, faces_2)

    def second_2(p):
        near = neighbours(first, fx, fy, fz, p, 2, 0)
        for q in range(2):
            x2[p, q] = (1.0 + KEEP - GAIN) * first[p, q] + GAIN * (b2[p, q] + near[q]) * dinv[p, q]

    loop(4, 3 * width - 4, second_2)

    totals = [jnp.zeros(shape, F32)] * depth
    cell_sums = [jnp.zeros(shape, F32)] * depth
    for p in range(5, 3 * width - 5):
        near = neighbours(x2, fx, fy, fz, p, 2, 0)
        j = (p - width) // 2
        for q in range(2):
            rest = b2[p, q] + near[q] - diag[p, q] * x2[p, q]
            r2[p, q] = rest
            if 0 <= j < depth:
                totals[j] = totals[j] + rest
                cell_sums[j] = cell_sums[j] + c2[p, q]
    zz, k = iota((128, 128), 0), iota((128, 128), 1)
    low_half = ones_where(k == zz // 2, 0.125)
    high_half = ones_where(k == zz // 2 + 64, 0.125)
    coarse = dot_exact(jnp.concatenate(totals, axis=0), low_half) + dot_exact(jnp.concatenate(cell_sums, axis=0), high_half)
    coarse = coarse.reshape(depth, 8, 128)
    for s in range(tall):
        sent[s] = coarse

    for p in range(3, 7):
        for q in range(2):
            r1h[p, q] = r1[p, q]
    edges = 8 * (depth - 1) * size
    for k in range(3):
        place = jnp.clip(n + (k - 1), 0, size - 1)

        def block(yb, j):
            start = pl.multiple_of((yb * size + place) * 24 + 8 * j, 8)
            return plane[pl.ds(start, 8), :]

        for j in range(2):
            start = edges + 8 * (2 * k + j)
            low = jnp.where(y == 0, below[start : start + 8], block(jnp.maximum(y - 1, 0), j))
            high = jnp.where(y == depth - 1, above[start : start + 8], block(jnp.minimum(y + 1, depth - 1), j))
            for q in range(2):
                r1h[1 + j, q, 4 * k : 4 * k + 4] = low[4 * q : 4 * q + 4]
                r1h[7 + j, q, 4 * k : 4 * k + 4] = high[4 * q : 4 * q + 4]
                r1h[1 + j, q, 12:16] = jnp.zeros((4, 128), F32)
                r1h[7 + j, q, 12:16] = jnp.zeros((4, 128), F32)
            if k != 1:
                tile = block(y, j)
                start = 2 if k == 0 else 8
                for x in range(2):
                    for q in range(2):
                        row = 4 * x + 2 * q
                        r1h[3 + 2 * j + x, q, start : start + 2] = tile[row : row + 2]


def sweeps(start, mid, out, source, fx, fa, fb, dinv, low, planes, count, axis):
    def one(p):
        near = neighbours(start, fx, fa, fb, p, count, axis)
        for q in range(count):
            mid[p, q] = (1.0 - 1.0 / THETA) * start[p, q] + (1.0 / THETA) * ((source[p, q] + near[q]) * dinv[p, q])

    loop(-1, planes + 1, lambda k: one(low + k))

    def two(p):
        near = neighbours(mid, fx, fa, fb, p, count, axis)
        for q in range(count):
            value = (1.0 - GAIN + KEEP) * mid[p, q] - KEEP * start[p, q]
            out(p, q, value + GAIN * ((source[p, q] + near[q]) * dinv[p, q]))

    loop(0, planes, lambda k: two(low + k))


def up_kernel(gathered, r1h, x2, r2, fx2, fy2, fz2, dinv2, c1, x1, fx1, fy1, fz1, dinv1, x0, b0, fx, fy, fz, dinv, result,
              c3, p3, r3, x3, i3, fx3, fy3, fz3, d3, s2, m2, f2, s1, m1, f1, s0, m0, f0, *, depth, tall):
    z, y, n = lax.axis_index("z"), lax.axis_index("y"), lax.axis_index("n")
    half = depth * tall // 2
    shape = (8, 128)
    row, lane = iota(shape, 0), iota(shape, 1)
    upper = lane >= 64

    def unpack(i):
        one, two = gathered[i], gathered[i + half]
        b = jnp.where(upper, pltpu.roll(two, 64, 1), one)
        c3[i + 1, 0] = jnp.where(upper, two, pltpu.roll(one, 64, 1))
        r3[i + 1, 0] = b
        p3[i + 1, 0] = b
        x3[i + 1, 0] = jnp.zeros(shape, F32)

    loop(0, half, unpack)

    def wrap(ref):
        ref[0, 0] = jnp.where(upper, pltpu.roll(ref[half, 0], 64, 1), 0.0)
        ref[half + 1, 0] = jnp.where(upper, 0.0, pltpu.roll(ref[1, 0], 64, 1))

    wrap(c3)
    scale = 0.5 / 64.0
    fx3[0, 0] = scale * (c3[0, 0] + c3[1, 0])

    def faces_3(p):
        gx, gy, gz, d = plane_faces([c3[p, 0]], [c3[p + 1, 0]], [fx3[p - 1, 0]], scale, 0, row == 7, row == 0, lane % 64 == 63, lane % 64 == 0)
        fx3[p, 0], fy3[p, 0], fz3[p, 0], d3[p, 0] = gx[0], gy[0], gz[0], d[0]

    loop(1, half + 1, faces_3)

    def whole(parts):
        total = functools.reduce(lambda a, b: a + b, parts)
        return jnp.sum(jnp.sum(total, axis=0, keepdims=True), axis=1, keepdims=True)

    def spread(values):
        parts = [jnp.zeros(shape, F32)] * 4
        for i, value in enumerate(values):
            parts[i % 4] = parts[i % 4] + value
        return whole(parts)

    start_norm = spread([r3[i + 1, 0] * r3[i + 1, 0] for i in range(half)])

    def iterate(_, norm):
        wrap(p3)
        products = []
        for p in range(1, half + 1):
            here = p3[p, 0]
            image = d3[p, 0] * here - neighbours(p3, fx3, fy3, fz3, p, 1, 0)[0]
            i3[p, 0] = image
            products.append(here * image)
        alpha = norm / spread(products)
        squares = []
        for p in range(1, half + 1):
            x3[p, 0] = x3[p, 0] + alpha * p3[p, 0]
            rest = r3[p, 0] - alpha * i3[p, 0]
            r3[p, 0] = rest
            squares.append(rest * rest)
        new = spread(squares)
        beta = new / norm
        for p in range(1, half + 1):
            p3[p, 0] = r3[p, 0] + beta * p3[p, 0]
        return new

    lax.fori_loop(0, COARSE_SWEEPS, iterate, start_norm)

    base = 2 * depth + 2 * y - 4
    tiles = []
    for j in range(5):
        place = jnp.clip(depth * z + y - 2 + j, 0, 2 * half - 1)
        high = place >= half
        tile = x3[jnp.where(high, place - half, place) + 1, 0]
        tiles.append(jnp.where(high, pltpu.roll(tile, 64, 1), tile))
    k, zz = iota((128, 128), 0), iota((128, 128), 1)
    fine = dot_exact(jnp.concatenate(tiles, axis=0), ones_where(k == zz // 2))
    for j in range(5):
        add = fine[8 * j : 8 * j + 8]
        for p in (base + 2 * j, base + 2 * j + 1):
            for q in range(2):
                s2[p, q] = jnp.where(dinv2[p, q] > 0.0, add, 0.0)

    def keep_2(p, q, value):
        f2[p, q] = x2[p, q] + value

    sweeps(s2, m2, keep_2, r2, fx2, fy2, fz2, dinv2, base + 2, 6, 2, 0)

    wide = jnp.concatenate([jnp.concatenate([f2[base + 2 + k, 0], f2[base + 2 + k, 1]], axis=0) for k in range(6)], axis=1)
    r, k = iota((16, 16), 0), iota((16, 16), 1)
    from_n = n + r // 4 - 1
    pick = ones_where((k == (r // 2) % 2 * 8 + from_n) & (from_n >= 0) & (from_n < 8))
    fine = chosen_dot(pick, wide)
    for p in range(10):
        k = (p + 1) // 2
        for q in range(2):
            s1[p, q] = jnp.where(c1[p, q] > 0.0, fine[:, 128 * k : 128 * k + 128], 0.0)

    def keep_1(p, q, value):
        f1[p, q] = x1[p, q] + value

    sweeps(s1, m1, keep_1, r1h, fx1, fz1, fy1, dinv1, 2, 6, 2, 1)

    wide = jnp.concatenate([f1[p, q] for p in range(2, 8) for q in range(2)], axis=1)
    r, k = iota((24, 16), 0), iota((24, 16), 1)
    fine = chosen_dot(ones_where(k == r // 2), wide)
    for p in range(6, 18):
        for q in range(4):
            j = 2 * (p // 2 - 3) + q // 2
            s0[p, q] = jnp.where(dinv[p, q] > 0.0, x0[p, q] + fine[:, 128 * j : 128 * j + 128], 0.0)

    def keep_0(p, q, value):
        start = (p - 8) * 8
        if not isinstance(start, int):
            start = pl.multiple_of(start, 8)
        f0[pl.ds(start, 8), 128 * q : 128 * q + 128] = value[8:16]

    sweeps(s0, m0, keep_0, b0, fx, fz, fy, dinv, 8, 8, 4, 1)
    k, z0 = iota((512, 512), 0), iota((512, 512), 1)
    back = ones_where(z0 == 4 * (k % 128) + k // 128)
    result[...] = dot_exact(f0[...], back).reshape(8, 8, 512)


def call(kernel, outs, *operands, scratch=(), limit=40):
    shapes = [jax.ShapeDtypeStruct(shape, F32) for shape in outs]
    return pl.pallas_call(
        kernel,
        out_shape=shapes,
        in_specs=[pl.BlockSpec(memory_space=pltpu.VMEM)] * len(operands),
        out_specs=[pl.BlockSpec(memory_space=pltpu.VMEM)] * len(outs),
        scratch_shapes=[pltpu.VMEM(shape, F32) for shape in scratch],
        compiler_params=pltpu.CompilerParams(vmem_limit_bytes=limit * 2**20),
    )(*operands)


def split(rhs_field, beta_cells):
    outs = [(16, 4, 8, 128), (SENT, 4, 8, 128), (SENT, 4, 8, 128)]
    return pl.pallas_call(
        split_kernel,
        out_shape=[jax.ShapeDtypeStruct(shape, F32) for shape in outs],
        in_specs=[pl.BlockSpec(memory_space=pltpu.HBM)] * 2,
        out_specs=[pl.BlockSpec(memory_space=pltpu.VMEM)] * 3,
        scratch_shapes=[pltpu.VMEM((8, 8, 512), F32)] * 2 + [pltpu.SemaphoreType.DMA((2,))],
        compiler_params=pltpu.CompilerParams(vmem_limit_bytes=40 * 2**20),
    )(pltpu.with_memory_space_constraint(rhs_field, pltpu.HBM), pltpu.with_memory_space_constraint(beta_cells, pltpu.HBM))


def ring(axis_size, step):
    return [(i, (i + step) % axis_size) for i in range(axis_size)]


def shards(rhs_field, beta_cells):
    tall, depth, size = lax.axis_size("z"), lax.axis_size("y"), lax.axis_size("n")
    wide, group = tall * depth, depth * size
    own, up, down = split(rhs_field, beta_cells)
    own_left = lax.ppermute(own, "n", ring(size, 1))
    own_right = lax.ppermute(own, "n", ring(size, -1))
    below = lax.ppermute(up, ("z", "y"), ring(wide, 1))
    above = lax.ppermute(down, ("z", "y"), ring(wide, -1))
    below, above, own_left, own_right = lax.optimization_barrier((below, above, own_left, own_right))
    corners = (2 * len(CORNERS), 4, 8, 128)
    to_right, to_left = call(functools.partial(corner_kernel, wide=wide), [corners] * 2, below, above)
    corner_left = lax.ppermute(to_right, "n", ring(size, 1))
    corner_right = lax.ppermute(to_left, "n", ring(size, -1))
    fine, coarse = (24, 4, 24, 128), (10, 2, 16, 128)
    outs = call(
        functools.partial(down_kernel, wide=wide, depth=depth),
        [(group, 3, 8, 128)] + [fine] * 6 + [coarse] * 7,
        own, below, above, own_left, own_right, corner_left, corner_right,
        scratch=[fine, fine, (18, 2, 32, 128), coarse, coarse, coarse, (4, 2, 8, 128)],
    )
    packed, level_zero = outs[0], outs[1:7]
    c1, x1, r1, *faces_1 = outs[7:14]
    plane = lax.all_to_all(packed, ("y", "n"), 0, 0)
    edge = group - size + 6
    up, down = call(functools.partial(edge_kernel, depth=depth), [(edge, 8, 128)] * 2, plane)
    below = lax.ppermute(up, "z", ring(tall, 1))
    above = lax.ppermute(down, "z", ring(tall, -1))
    slab = (6 * depth, 2, 8, 128)
    outs = call(
        functools.partial(middle_kernel, depth=depth, tall=tall),
        [(tall, depth, 8, 128)] + [slab] * 6 + [coarse],
        plane.reshape(group * 24, 128), below.reshape(edge * 8, 128), above.reshape(edge * 8, 128), r1,
        scratch=[slab, slab, slab, slab],
    )
    sent, level_two, r1h = outs[0], outs[1:7], outs[7]
    gathered = lax.all_to_all(sent, "z", 0, 0)
    packed_3 = (wide // 2 + 2, 1, 8, 128)
    (result,) = call(
        functools.partial(up_kernel, depth=depth, tall=tall),
        [(8, 8, 512)],
        gathered.reshape(wide, 8, 128), r1h, *level_two, c1, x1, *faces_1, *level_zero,
        scratch=[packed_3] * 9 + [slab] * 3 + [coarse] * 3 + [fine] * 2 + [(64, 512)],
    )
    return result


def solution(mesh):
    wide, size = mesh.shape["wide"], mesh.shape["narrow"]
    inner = Mesh(mesh.devices.reshape(wide // 4, 4, size), ("z", "y", "n"))
    spec = P(("z", "y"), "n", None)
    return jax.shard_map(shards, mesh=inner, in_specs=(spec, spec), out_specs=spec, check_vma=False)
```

```python
import functools

import jax
import jax.numpy as jnp
from jax import lax
from jax.experimental import pallas as pl
from jax.experimental.pallas import tpu as pltpu
from jax.sharding import Mesh, PartitionSpec as P

F32 = jnp.float32
BF16 = jnp.bfloat16

THETA = 0.5 * (2.0 + 0.25)
DELTA = 0.5 * (2.0 - 0.25)
SIGMA = THETA / DELTA
RHO_0 = 1.0 / SIGMA
RHO_1 = 1.0 / (2.0 * SIGMA - RHO_0)
KEEP = RHO_1 * RHO_0
GAIN = 2.0 * RHO_1 / DELTA
COARSE_SWEEPS = 8


def dot_exact(values, chooser):
    high = values.astype(BF16)
    rest = values - high.astype(F32)
    middle = rest.astype(BF16)
    low = (rest - middle.astype(F32)).astype(BF16)
    rows = values.shape[0]
    out = jnp.dot(jnp.concatenate([high, middle, low], axis=0), chooser, preferred_element_type=F32)
    return out[:rows] + out[rows : 2 * rows] + out[2 * rows :]


def chosen_dot(chooser, values):
    high = values.astype(BF16)
    rest = values - high.astype(F32)
    middle = rest.astype(BF16)
    low = (rest - middle.astype(F32)).astype(BF16)
    out = jnp.dot(chooser, high, preferred_element_type=F32)
    out = out + jnp.dot(chooser, middle, preferred_element_type=F32)
    return out + jnp.dot(chooser, low, preferred_element_type=F32)


def iota(shape, dim):
    return lax.broadcasted_iota(jnp.int32, shape, dim)


def ones_where(mask, value=1.0):
    return jnp.where(mask, value, 0.0).astype(BF16)


def shift(values, step, axis):
    size = values.shape[axis]
    return pltpu.roll(values, (-step) % size, axis)


def plane_faces(c, c_next, fx_before, scale, axis, last, first, last_b=None, first_b=None):
    count, other = len(c), 1 - axis
    fx = [scale * (c[q] + c_next[q]) for q in range(count)]
    after = [c[q + 1] if q + 1 < count else jnp.where(last, 0.0, shift(c[0], 1, axis)) for q in range(count)]
    fa = [scale * (c[q] + after[q]) for q in range(count)]
    lowest = jnp.where(first, scale * c[0], shift(fa[-1], -1, axis))
    fb, diagonal = [], []
    for q in range(count):
        beside = shift(c[q], 1, other)
        if last_b is not None:
            beside = jnp.where(last_b, 0.0, beside)
        face = scale * (c[q] + beside)
        face_before = shift(face, -1, other)
        if first_b is not None:
            face_before = jnp.where(first_b, scale * c[q], face_before)
        diagonal.append(fx[q] + fx_before[q] + face + face_before + fa[q] + (fa[q - 1] if q else lowest))
        fb.append(face if last_b is None else jnp.where(last_b, 0.0, face))
    fa[-1] = jnp.where(last, 0.0, fa[-1])
    return fx, fa, fb, diagonal


def neighbours(u, fx, fa, fb, p, count, axis):
    other = 1 - axis
    here = [u[p, q] for q in range(count)]
    faces = [fa[p, q] for q in range(count)]
    out = []
    for q in range(count):
        face = fb[p, q]
        total = fx[p, q] * u[p + 1, q] + fx[p - 1, q] * u[p - 1, q]
        total = total + face * shift(here[q], 1, other) + shift(face * here[q], -1, other)
        if q + 1 < count:
            total = total + faces[q] * here[q + 1]
        else:
            total = total + faces[q] * shift(here[0], 1, axis)
        if q > 0:
            total = total + faces[q - 1] * here[q - 1]
        else:
            total = total + shift(faces[-1] * here[-1], -1, axis)
        out.append(total)
    return out


def loop(low, high, body):
    for k in range(high - low):
        body(low + k)


def inverse(c, diagonal):
    return jnp.where(c > 0.0, 1.0 / diagonal, 0.0)


C_LOW, B_LOW = 7, 6
SENT = C_LOW + B_LOW

CORNERS = (
    (0, 1, 0, 0), (0, 2, 0, 0), (0, 3, 7, 2), (0, 4, 6, 3), (0, 5, 0, 0),
    (1, 1, 6, 2), (1, 2, 0, 0), (1, 3, 5, 3), (1, 4, 0, 0),
)


def split_kernel(rhs_hbm, beta_hbm, own, up, down, rhs, beta, sems):
    copies = [
        pltpu.make_async_copy(beta_hbm, beta, sems.at[0]),
        pltpu.make_async_copy(rhs_hbm, rhs, sems.at[1]),
    ]
    for copy in copies:
        copy.start()
    z = iota((512, 512), 0)
    k = iota((512, 512), 1)
    chooser = ones_where(z == 4 * (k % 128) + k // 128)
    for field, source in enumerate((beta, rhs)):
        copies[field].wait()
        out = dot_exact(source[...].reshape(64, 512), chooser)
        for x in range(8):
            for q in range(4):
                tile = out[8 * x : 8 * x + 8, 128 * q : 128 * q + 128]
                own[8 * field + x, q] = tile
                width = (C_LOW, B_LOW)[field]
                start = (0, C_LOW)[field]
                if x >= 8 - width:
                    up[start + x - (8 - width), q] = tile
                if x < width:
                    down[start + x, q] = tile


def side_index(side, field, distance):
    width, start = (C_LOW, B_LOW)[field], (0, C_LOW)[field]
    return start + (width - distance if side == 0 else distance - 1)


def corner_kernel(planes, right, left, *, side, wide):
    index = lax.axis_index("z") * lax.axis_size("y") + lax.axis_index("y")
    inside = index > 0 if side == 0 else index < wide - 1
    keep = jnp.where(inside, 1.0, 0.0).astype(F32)
    row = iota((8, 128), 0)
    for t, (field, one, two, rows) in enumerate(CORNERS):
        for q in range(4):
            tile = planes[side_index(side, field, one), q]
            to_right = to_left = tile
            if two:
                other = planes[side_index(side, field, two), q]
                to_right = jnp.where(row >= rows, tile, pltpu.roll(other, rows, 0))
                to_left = jnp.where(row < 8 - rows, tile, pltpu.roll(other, 8 - rows, 0))
            if field == 0:
                to_right, to_left = to_right * keep, to_left * keep
            right[t, q] = to_right
            left[t, q] = to_left


def down_kernel(own, below, above, own_left, own_right, left_0, right_0, left_1, right_1, packed, x0, b0, fx, fy, fz, dinv, c1, x1, r1, fx1, fy1, fz1, dinv1, diag, first, sums, diag1, first1, b1, parts, *, wide, depth):
    n = lax.axis_index("n")
    index = lax.axis_index("z") * lax.axis_size("y") + lax.axis_index("y")
    keep_wide = [jnp.where(index > 0, 1.0, 0.0).astype(F32), jnp.where(index < wide - 1, 1.0, 0.0).astype(F32)]
    keep_left = jnp.where(n > 0, 1.0, 0.0).astype(F32)
    keep_right = jnp.where(n < lax.axis_size("n") - 1, 1.0, 0.0).astype(F32)
    lane = iota((24, 128), 1)
    last, begin = lane == 127, lane == 0

    corner = {}
    for t, (field, one, two, rows) in enumerate(CORNERS):
        corner[field, one] = (t, 0)
        if two:
            corner[field, two] = (t, rows)

    def plane(field, p, keep_0, keep_1):
        x = p - 8
        out = []
        for q in range(4):
            if 0 <= x < 8:
                parts = [own_left[8 * field + x, q], own[8 * field + x, q], own_right[8 * field + x, q]]
            else:
                side, distance = (0, -x) if x < 0 else (1, x - 7)
                t, rows = corner[field, distance]
                beside = ((left_0, right_0), (left_1, right_1))[side]
                parts = [beside[0][t, q], (below, above)[side][side_index(side, field, distance), q], beside[1][t, q]]
                if rows:
                    parts[0] = pltpu.roll(parts[0], 8 - rows, 0)
                    parts[2] = pltpu.roll(parts[2], rows, 0)
                if field == 0:
                    parts[1] = parts[1] * keep_wide[side]
            out.append(jnp.concatenate([parts[0] * keep_0, parts[1], parts[2] * keep_1] if field == 0 else parts, axis=0))
        return out

    def cells(p):
        return plane(0, p, keep_left, keep_right)

    def source(p):
        return plane(1, p, None, None)

    before, after = cells(1), cells(2)
    for q in range(4):
        fx[1, q] = 0.5 * (before[q] + after[q])

    def faces_0(p):
        c, c_next, b = cells(p), cells(p + 1), source(p)
        gx, gz, gy, d = plane_faces(c, c_next, [fx[p - 1, q] for q in range(4)], 0.5, 1, last, begin)
        for q in range(4):
            fx[p, q], fy[p, q], fz[p, q], diag[p, q] = gx[q], gy[q], gz[q], d[q]
            inv = inverse(c[q], d[q])
            dinv[p, q] = inv
            b0[p, q] = b[q]
            first[p, q] = b[q] * inv * (1.0 / THETA)

    loop(2, 22, faces_0)

    def second_0(p):
        near = neighbours(first, fx, fz, fy, p, 4, 1)
        for q in range(4):
            x0[p, q] = (1.0 + KEEP - GAIN) * first[p, q] + GAIN * (b0[p, q] + near[q]) * dinv[p, q]

    loop(3, 21, second_0)

    def residual_0(k):
        total = [jnp.zeros((24, 128), F32)] * 2
        for p in (4 + 2 * k, 5 + 2 * k):
            near = neighbours(x0, fx, fz, fy, p, 4, 1)
            for q in range(4):
                total[q // 2] = total[q // 2] + (b0[p, q] + near[q] - diag[p, q] * x0[p, q])
        for q in range(2):
            sums[k, q, 0:24] = total[q]
            sums[k, q, 24:32] = jnp.zeros((8, 128), F32)

    loop(0, 8, residual_0)

    def cells_1(k):
        one, two = cells(2 + 2 * k), cells(3 + 2 * k)
        for q in range(2):
            sums[8 + k, q, 0:24] = (one[2 * q] + one[2 * q + 1]) + (two[2 * q] + two[2 * q + 1])
            sums[8 + k, q, 24:32] = jnp.zeros((8, 128), F32)

    loop(0, 10, cells_1)

    def halve(k, q):
        return 0.125 * (sums[k, q, pl.ds(0, 16, stride=2), :] + sums[k, q, pl.ds(1, 16, stride=2), :])

    for q in range(2):
        loop(0, 8, lambda k, q=q: b1.__setitem__((k + 1, q), halve(k, q)))
        loop(0, 10, lambda k, q=q: c1.__setitem__((k, q), halve(8 + k, q)))

    lane = iota((16, 128), 1)
    last_1, begin_1 = lane == 127, lane == 0
    for q in range(2):
        fx1[0, q] = 0.125 * (c1[0, q] + c1[1, q])

    def faces_1(p):
        c, c_next = [c1[p, q] for q in range(2)], [c1[p + 1, q] for q in range(2)]
        gx, gz, gy, d = plane_faces(c, c_next, [fx1[p - 1, q] for q in range(2)], 0.125, 1, last_1, begin_1)
        for q in range(2):
            fx1[p, q], fy1[p, q], fz1[p, q], diag1[p, q] = gx[q], gy[q], gz[q], d[q]
            inv = inverse(c[q], d[q])
            dinv1[p, q] = inv
            first1[p, q] = b1[p, q] * inv * (1.0 / THETA)

    loop(1, 9, faces_1)

    def second_1(p):
        near = neighbours(first1, fx1, fz1, fy1, p, 2, 1)
        for q in range(2):
            x1[p, q] = (1.0 + KEEP - GAIN) * first1[p, q] + GAIN * (b1[p, q] + near[q]) * dinv1[p, q]

    loop(2, 8, second_1)

    y, size = lax.axis_index("y"), lax.axis_size("n")
    for x in range(2):
        total = jnp.zeros((16, 128), F32)
        cell = jnp.zeros((16, 128), F32)
        for p in (3 + 2 * x, 4 + 2 * x):
            near = neighbours(x1, fx1, fz1, fy1, p, 2, 1)
            for q in range(2):
                rest = b1[p, q] + near[q] - diag1[p, q] * x1[p, q]
                r1[p, q] = rest
                total = total + rest
                cell = cell + c1[p, q]
                place = p - 3
                parts[place // 2, place % 2, 4 * q : 4 * q + 4] = rest[4:8]
                row = 4 * (place % 2) + 2 * q
                parts[2, place // 2, row : row + 2] = rest[6:8]
                parts[3, place // 2, row : row + 2] = rest[4:6]
        total = 0.125 * (total + shift(total, 1, 0))
        cell = 0.125 * (cell + shift(cell, 1, 0))
        for yy in range(2):
            packed[0, 2, 2 * x + yy : 2 * x + yy + 1] = total[4 + 2 * yy : 5 + 2 * yy]
            packed[0, 2, 4 + 2 * x + yy : 5 + 2 * x + yy] = cell[4 + 2 * yy : 5 + 2 * yy]

    level_two = packed[0, 2]
    for y_to in range(depth):
        ahead = (y_to - y + depth) % depth
        for n_to in range(size):
            beside = jnp.where(n_to > n, 2, 3)
            part = jnp.where(ahead == 0, beside, jnp.where(ahead == 1, 1, 0))
            s = y_to * size + n_to
            packed[s, 0] = parts[part, 0]
            packed[s, 1] = parts[part, 1]
            packed[s, 2] = level_two


def edge_kernel(plane, up, down, *, depth):
    n = lax.axis_index("n")
    size = lax.axis_size("n")

    count = (depth - 1) * size
    for s in range(count):
        up[s] = plane[size + s, 2]
        down[s] = plane[s, 2]
    for k in range(3):
        place = jnp.clip(n + (k - 1), 0, size - 1)
        for j in range(2):
            up[count + 2 * k + j] = plane[count + place, j]
            down[count + 2 * k + j] = plane[place, j]


def middle_kernel(plane, below, above, r1, sent, x2, r2, fx, fy, fz, dinv, r1h, b2, c2, diag, first, half, *, depth, tall):
    z, y, n = lax.axis_index("z"), lax.axis_index("y"), lax.axis_index("n")
    size = lax.axis_size("n")
    keep_low = jnp.where(z > 0, 1.0, 0.0).astype(F32)
    keep_high = jnp.where(z < tall - 1, 1.0, 0.0).astype(F32)
    width = 2 * depth
    for yb in range(depth):
        for x in range(2):
            for yy in range(2):
                r = 2 * x + yy
                place = 2 * yb + x
                own = yb * size * 24 + 16 + r
                b2[width + place, yy] = plane[pl.ds(own, 8, stride=24), :]
                c2[width + place, yy] = plane[pl.ds(own + 4, 8, stride=24), :]
                if yb > 0:
                    edge = (yb - 1) * size * 8 + r
                    b2[place, yy] = below[pl.ds(edge, 8, stride=8), :]
                    c2[place, yy] = below[pl.ds(edge + 4, 8, stride=8), :] * keep_low
                if yb < depth - 1:
                    edge = yb * size * 8 + r
                    b2[2 * width + place, yy] = above[pl.ds(edge, 8, stride=8), :]
                    c2[2 * width + place, yy] = above[pl.ds(edge + 4, 8, stride=8), :] * keep_high

    scale = 0.5 / 16.0
    shape = (8, 128)
    row, lane = iota(shape, 0), iota(shape, 1)
    last, begin, last_b, begin_b = row == 7, row == 0, lane == 127, lane == 0
    for q in range(2):
        fx[2, q] = scale * (c2[2, q] + c2[3, q])

    def faces_2(p):
        c, c_next = [c2[p, q] for q in range(2)], [c2[p + 1, q] for q in range(2)]
        gx, gy, gz, d = plane_faces(c, c_next, [fx[p - 1, q] for q in range(2)], scale, 0, last, begin, last_b, begin_b)
        for q in range(2):
            fx[p, q], fy[p, q], fz[p, q], diag[p, q] = gx[q], gy[q], gz[q], d[q]
            inv = inverse(c[q], d[q])
            dinv[p, q] = inv
            first[p, q] = b2[p, q] * inv * (1.0 / THETA)

    loop(3, 3 * width - 3, faces_2)

    def second_2(p):
        near = neighbours(first, fx, fy, fz, p, 2, 0)
        for q in range(2):
            x2[p, q] = (1.0 + KEEP - GAIN) * first[p, q] + GAIN * (b2[p, q] + near[q]) * dinv[p, q]

    loop(4, 3 * width - 4, second_2)

    totals = [jnp.zeros(shape, F32)] * depth
    cell_sums = [jnp.zeros(shape, F32)] * depth
    for p in range(5, 3 * width - 5):
        near = neighbours(x2, fx, fy, fz, p, 2, 0)
        j = (p - width) // 2
        for q in range(2):
            rest = b2[p, q] + near[q] - diag[p, q] * x2[p, q]
            r2[p, q] = rest
            if 0 <= j < depth:
                totals[j] = totals[j] + rest
                cell_sums[j] = cell_sums[j] + c2[p, q]
    zz, k = iota((128, 128), 0), iota((128, 128), 1)
    low_half = ones_where(k == zz // 2, 0.125)
    high_half = ones_where(k == zz // 2 + 64, 0.125)
    coarse = dot_exact(jnp.concatenate(totals, axis=0), low_half) + dot_exact(jnp.concatenate(cell_sums, axis=0), high_half)
    for j in range(depth):
        half[j // 2, j % 2] = coarse[8 * j : 8 * j + 8]
    mine = half[n % 2]
    for s in range(tall):
        sent[s] = mine

    for p in range(3, 7):
        for q in range(2):
            r1h[p, q] = r1[p, q]
    edges = 8 * (depth - 1) * size
    for k in range(3):
        place = jnp.clip(n + (k - 1), 0, size - 1)

        def block(yb, j):
            start = pl.multiple_of((yb * size + place) * 24 + 8 * j, 8)
            return plane[pl.ds(start, 8), :]

        for j in range(2):
            start = edges + 8 * (2 * k + j)
            low = jnp.where(y == 0, below[start : start + 8], block(jnp.maximum(y - 1, 0), j))
            high = jnp.where(y == depth - 1, above[start : start + 8], block(jnp.minimum(y + 1, depth - 1), j))
            for q in range(2):
                r1h[1 + j, q, 4 * k : 4 * k + 4] = low[4 * q : 4 * q + 4]
                r1h[7 + j, q, 4 * k : 4 * k + 4] = high[4 * q : 4 * q + 4]
                r1h[1 + j, q, 12:16] = jnp.zeros((4, 128), F32)
                r1h[7 + j, q, 12:16] = jnp.zeros((4, 128), F32)
            if k != 1:
                tile = block(y, j)
                start = 2 if k == 0 else 8
                for x in range(2):
                    for q in range(2):
                        row = 4 * x + 2 * q
                        r1h[3 + 2 * j + x, q, start : start + 2] = tile[row : row + 2]


def sweeps(start, mid, out, source, fx, fa, fb, dinv, low, planes, count, axis):
    def one(p):
        near = neighbours(start, fx, fa, fb, p, count, axis)
        for q in range(count):
            mid[p, q] = (1.0 - 1.0 / THETA) * start[p, q] + (1.0 / THETA) * ((source[p, q] + near[q]) * dinv[p, q])

    loop(-1, planes + 1, lambda k: one(low + k))

    def two(p):
        near = neighbours(mid, fx, fa, fb, p, count, axis)
        for q in range(count):
            value = (1.0 - GAIN + KEEP) * mid[p, q] - KEEP * start[p, q]
            out(p, q, value + GAIN * ((source[p, q] + near[q]) * dinv[p, q]))

    loop(0, planes, lambda k: two(low + k))


def up_kernel(gathered, r1h, x2, r2, fx2, fy2, fz2, dinv2, c1, x1, fx1, fy1, fz1, dinv1, x0, b0, fx, fy, fz, dinv, result,
              c3, p3, r3, x3, i3, fx3, fy3, fz3, d3, s2, m2, f2, s1, m1, f1, s0, m0, f0, *, depth, tall):
    z, y, n = lax.axis_index("z"), lax.axis_index("y"), lax.axis_index("n")
    half = depth * tall // 2
    shape = (8, 128)
    row, lane = iota(shape, 0), iota(shape, 1)
    upper = lane >= 64

    def unpack(i):
        one, two = [gathered[j % depth // 2, j // depth, j % 2] for j in (i, i + half)]
        b = jnp.where(upper, pltpu.roll(two, 64, 1), one)
        c3[i + 1, 0] = jnp.where(upper, two, pltpu.roll(one, 64, 1))
        r3[i + 1, 0] = b
        p3[i + 1, 0] = b
        x3[i + 1, 0] = jnp.zeros(shape, F32)

    loop(0, half, unpack)

    def wrap(ref):
        ref[0, 0] = jnp.where(upper, pltpu.roll(ref[half, 0], 64, 1), 0.0)
        ref[half + 1, 0] = jnp.where(upper, 0.0, pltpu.roll(ref[1, 0], 64, 1))

    wrap(c3)
    scale = 0.5 / 64.0
    fx3[0, 0] = scale * (c3[0, 0] + c3[1, 0])

    def faces_3(p):
        gx, gy, gz, d = plane_faces([c3[p, 0]], [c3[p + 1, 0]], [fx3[p - 1, 0]], scale, 0, row == 7, row == 0, lane % 64 == 63, lane % 64 == 0)
        fx3[p, 0], fy3[p, 0], fz3[p, 0], d3[p, 0] = gx[0], gy[0], gz[0], d[0]

    loop(1, half + 1, faces_3)

    def whole(parts):
        total = functools.reduce(lambda a, b: a + b, parts)
        return jnp.sum(jnp.sum(total, axis=0, keepdims=True), axis=1, keepdims=True)

    def spread(values):
        parts = [jnp.zeros(shape, F32)] * 4
        for i, value in enumerate(values):
            parts[i % 4] = parts[i % 4] + value
        return whole(parts)

    start_norm = spread([r3[i + 1, 0] * r3[i + 1, 0] for i in range(half)])

    def iterate(norm):
        wrap(p3)
        products = []
        for p in range(1, half + 1):
            here = p3[p, 0]
            image = d3[p, 0] * here - neighbours(p3, fx3, fy3, fz3, p, 1, 0)[0]
            i3[p, 0] = image
            products.append(here * image)
        alpha = norm / spread(products)
        squares = []
        for p in range(1, half + 1):
            x3[p, 0] = x3[p, 0] + alpha * p3[p, 0]
            rest = r3[p, 0] - alpha * i3[p, 0]
            r3[p, 0] = rest
            squares.append(rest * rest)
        new = spread(squares)
        beta = new / norm
        for p in range(1, half + 1):
            p3[p, 0] = r3[p, 0] + beta * p3[p, 0]
        return new

    norm = start_norm
    for _ in range(COARSE_SWEEPS):
        norm = iterate(norm)

    base = 2 * depth + 2 * y - 4
    tiles = []
    for j in range(5):
        place = jnp.clip(depth * z + y - 2 + j, 0, 2 * half - 1)
        high = place >= half
        tile = x3[jnp.where(high, place - half, place) + 1, 0]
        tiles.append(jnp.where(high, pltpu.roll(tile, 64, 1), tile))
    k, zz = iota((128, 128), 0), iota((128, 128), 1)
    fine = dot_exact(jnp.concatenate(tiles, axis=0), ones_where(k == zz // 2))
    for j in range(5):
        add = fine[8 * j : 8 * j + 8]
        for p in (base + 2 * j, base + 2 * j + 1):
            for q in range(2):
                s2[p, q] = jnp.where(dinv2[p, q] > 0.0, add, 0.0)

    def keep_2(p, q, value):
        f2[p, q] = x2[p, q] + value

    sweeps(s2, m2, keep_2, r2, fx2, fy2, fz2, dinv2, base + 2, 6, 2, 0)

    wide = jnp.concatenate([jnp.concatenate([f2[base + 2 + k, 0], f2[base + 2 + k, 1]], axis=0) for k in range(6)], axis=1)
    r, k = iota((16, 16), 0), iota((16, 16), 1)
    from_n = n + r // 4 - 1
    pick = ones_where((k == (r // 2) % 2 * 8 + from_n) & (from_n >= 0) & (from_n < 8))
    fine = chosen_dot(pick, wide)
    for p in range(10):
        k = (p + 1) // 2
        for q in range(2):
            s1[p, q] = jnp.where(c1[p, q] > 0.0, fine[:, 128 * k : 128 * k + 128], 0.0)

    def keep_1(p, q, value):
        f1[p, q] = x1[p, q] + value

    sweeps(s1, m1, keep_1, r1h, fx1, fz1, fy1, dinv1, 2, 6, 2, 1)

    wide = jnp.concatenate([f1[p, q] for p in range(2, 8) for q in range(2)], axis=1)
    r, k = iota((24, 16), 0), iota((24, 16), 1)
    fine = chosen_dot(ones_where(k == r // 2), wide)
    for p in range(6, 18):
        for q in range(4):
            j = 2 * (p // 2 - 3) + q // 2
            s0[p, q] = jnp.where(dinv[p, q] > 0.0, x0[p, q] + fine[:, 128 * j : 128 * j + 128], 0.0)

    def keep_0(p, q, value):
        start = (p - 8) * 8
        if not isinstance(start, int):
            start = pl.multiple_of(start, 8)
        f0[pl.ds(start, 8), 128 * q : 128 * q + 128] = value[8:16]

    sweeps(s0, m0, keep_0, b0, fx, fz, fy, dinv, 8, 8, 4, 1)
    k, z0 = iota((512, 512), 0), iota((512, 512), 1)
    back = ones_where(z0 == 4 * (k % 128) + k // 128)
    result[...] = dot_exact(f0[...], back).reshape(8, 8, 512)


def call(kernel, outs, *operands, scratch=(), limit=40):
    shapes = [jax.ShapeDtypeStruct(shape, F32) for shape in outs]
    return pl.pallas_call(
        kernel,
        out_shape=shapes,
        in_specs=[pl.BlockSpec(memory_space=pltpu.VMEM)] * len(operands),
        out_specs=[pl.BlockSpec(memory_space=pltpu.VMEM)] * len(outs),
        scratch_shapes=[pltpu.VMEM(shape, F32) for shape in scratch],
        compiler_params=pltpu.CompilerParams(vmem_limit_bytes=limit * 2**20),
    )(*operands)


def split(rhs_field, beta_cells):
    outs = [(16, 4, 8, 128), (SENT, 4, 8, 128), (SENT, 4, 8, 128)]
    return pl.pallas_call(
        split_kernel,
        out_shape=[jax.ShapeDtypeStruct(shape, F32) for shape in outs],
        in_specs=[pl.BlockSpec(memory_space=pltpu.HBM)] * 2,
        out_specs=[pl.BlockSpec(memory_space=pltpu.VMEM)] * 3,
        scratch_shapes=[pltpu.VMEM((8, 8, 512), F32)] * 2 + [pltpu.SemaphoreType.DMA((2,))],
        compiler_params=pltpu.CompilerParams(vmem_limit_bytes=40 * 2**20),
    )(pltpu.with_memory_space_constraint(rhs_field, pltpu.HBM), pltpu.with_memory_space_constraint(beta_cells, pltpu.HBM))


def ring(axis_size, step):
    return [(i, (i + step) % axis_size) for i in range(axis_size)]


def shards(rhs_field, beta_cells):
    tall, depth, size = lax.axis_size("z"), lax.axis_size("y"), lax.axis_size("n")
    wide, group = tall * depth, depth * size
    own, up, down = split(rhs_field, beta_cells)
    own_left = lax.ppermute(own, "n", ring(size, 1))
    own_right = lax.ppermute(own, "n", ring(size, -1))
    below = lax.ppermute(up, ("z", "y"), ring(wide, 1))
    above = lax.ppermute(down, ("z", "y"), ring(wide, -1))
    corners = []
    for side, planes in enumerate((below, above)):
        to_right, to_left = call(
            functools.partial(corner_kernel, side=side, wide=wide), [(len(CORNERS), 4, 8, 128)] * 2, planes
        )
        corners += [lax.ppermute(to_right, "n", ring(size, 1)), lax.ppermute(to_left, "n", ring(size, -1))]
    fine, coarse = (24, 4, 24, 128), (10, 2, 16, 128)
    outs = call(
        functools.partial(down_kernel, wide=wide, depth=depth),
        [(group, 3, 8, 128)] + [fine] * 6 + [coarse] * 7,
        own, below, above, own_left, own_right, *corners,
        scratch=[fine, fine, (18, 2, 32, 128), coarse, coarse, coarse, (4, 2, 8, 128)],
    )
    packed, level_zero = outs[0], outs[1:7]
    c1, x1, r1, *faces_1 = outs[7:14]
    plane = lax.all_to_all(packed, ("y", "n"), 0, 0)
    edge = group - size + 6
    up, down = call(functools.partial(edge_kernel, depth=depth), [(edge, 8, 128)] * 2, plane)
    below = lax.ppermute(up, "z", ring(tall, 1))
    above = lax.ppermute(down, "z", ring(tall, -1))
    slab = (6 * depth, 2, 8, 128)
    outs = call(
        functools.partial(middle_kernel, depth=depth, tall=tall),
        [(tall, depth // 2, 8, 128)] + [slab] * 6 + [coarse],
        plane.reshape(group * 24, 128), below.reshape(edge * 8, 128), above.reshape(edge * 8, 128), r1,
        scratch=[slab, slab, slab, slab, (2, depth // 2, 8, 128)],
    )
    sent, level_two, r1h = outs[0], outs[1:7], outs[7]
    gathered = lax.all_to_all(sent, "z", 0, 0)
    pairs = [[2 * i, 2 * i + 1] for i in range(size // 2)]
    gathered = lax.all_gather(gathered, "n", axis_index_groups=pairs)
    packed_3 = (wide // 2 + 2, 1, 8, 128)
    (result,) = call(
        functools.partial(up_kernel, depth=depth, tall=tall),
        [(8, 8, 512)],
        gathered, r1h, *level_two, c1, x1, *faces_1, *level_zero,
        scratch=[packed_3] * 9 + [slab] * 3 + [coarse] * 3 + [fine] * 2 + [(64, 512)],
    )
    return result


def solution(mesh):
    wide, size = mesh.shape["wide"], mesh.shape["narrow"]
    inner = Mesh(mesh.devices.reshape(wide // 4, 4, size), ("z", "y", "n"))
    spec = P(("z", "y"), "n", None)
    return jax.shard_map(shards, mesh=inner, in_specs=(spec, spec), out_specs=spec, check_vma=False)
```

```python
import functools

import jax
import jax.numpy as jnp
from jax import lax
from jax.experimental import pallas as pl
from jax.experimental.pallas import tpu as pltpu
from jax.sharding import Mesh, PartitionSpec as P

F32 = jnp.float32
BF16 = jnp.bfloat16

THETA = 0.5 * (2.0 + 0.25)
DELTA = 0.5 * (2.0 - 0.25)
SIGMA = THETA / DELTA
RHO_0 = 1.0 / SIGMA
RHO_1 = 1.0 / (2.0 * SIGMA - RHO_0)
KEEP = RHO_1 * RHO_0
GAIN = 2.0 * RHO_1 / DELTA
COARSE_SWEEPS = 8


def dot_exact(values, chooser):
    high = values.astype(BF16)
    rest = values - high.astype(F32)
    middle = rest.astype(BF16)
    low = (rest - middle.astype(F32)).astype(BF16)
    rows = values.shape[0]
    out = jnp.dot(jnp.concatenate([high, middle, low], axis=0), chooser, preferred_element_type=F32)
    return out[:rows] + out[rows : 2 * rows] + out[2 * rows :]


def chosen_dot(chooser, values):
    high = values.astype(BF16)
    rest = values - high.astype(F32)
    middle = rest.astype(BF16)
    low = (rest - middle.astype(F32)).astype(BF16)
    out = jnp.dot(chooser, high, preferred_element_type=F32)
    out = out + jnp.dot(chooser, middle, preferred_element_type=F32)
    return out + jnp.dot(chooser, low, preferred_element_type=F32)


def iota(shape, dim):
    return lax.broadcasted_iota(jnp.int32, shape, dim)


def ones_where(mask, value=1.0):
    return jnp.where(mask, value, 0.0).astype(BF16)


def shift(values, step, axis):
    size = values.shape[axis]
    return pltpu.roll(values, (-step) % size, axis)


def plane_faces(c, c_next, fx_before, scale, axis, last, first, last_b=None, first_b=None):
    count, other = len(c), 1 - axis
    fx = [scale * (c[q] + c_next[q]) for q in range(count)]
    after = [c[q + 1] if q + 1 < count else jnp.where(last, 0.0, shift(c[0], 1, axis)) for q in range(count)]
    fa = [scale * (c[q] + after[q]) for q in range(count)]
    lowest = jnp.where(first, scale * c[0], shift(fa[-1], -1, axis))
    fb, diagonal = [], []
    for q in range(count):
        beside = shift(c[q], 1, other)
        if last_b is not None:
            beside = jnp.where(last_b, 0.0, beside)
        face = scale * (c[q] + beside)
        face_before = shift(face, -1, other)
        if first_b is not None:
            face_before = jnp.where(first_b, scale * c[q], face_before)
        diagonal.append(fx[q] + fx_before[q] + face + face_before + fa[q] + (fa[q - 1] if q else lowest))
        fb.append(face if last_b is None else jnp.where(last_b, 0.0, face))
    fa[-1] = jnp.where(last, 0.0, fa[-1])
    return fx, fa, fb, diagonal


def neighbours(u, fx, fa, fb, p, count, axis):
    other = 1 - axis
    here = [u[p, q] for q in range(count)]
    faces = [fa[p, q] for q in range(count)]
    out = []
    for q in range(count):
        face = fb[p, q]
        total = fx[p, q] * u[p + 1, q] + fx[p - 1, q] * u[p - 1, q]
        total = total + face * shift(here[q], 1, other) + shift(face * here[q], -1, other)
        if q + 1 < count:
            total = total + faces[q] * here[q + 1]
        else:
            total = total + faces[q] * shift(here[0], 1, axis)
        if q > 0:
            total = total + faces[q - 1] * here[q - 1]
        else:
            total = total + shift(faces[-1] * here[-1], -1, axis)
        out.append(total)
    return out


def loop(low, high, body):
    for k in range(high - low):
        body(low + k)


def inverse(c, diagonal):
    return jnp.where(c > 0.0, 1.0 / diagonal, 0.0)


C_LOW, B_LOW = 7, 6
SENT = C_LOW + B_LOW

CORNERS = (
    (0, 1, 0, 0), (0, 2, 0, 0), (0, 3, 7, 2), (0, 4, 6, 3), (0, 5, 0, 0),
    (1, 1, 6, 2), (1, 2, 0, 0), (1, 3, 5, 3), (1, 4, 0, 0),
)


def split_kernel(rhs_hbm, beta_hbm, own, pair, other, rhs, beta, sems):
    copies = [
        pltpu.make_async_copy(beta_hbm, beta, sems.at[0]),
        pltpu.make_async_copy(rhs_hbm, rhs, sems.at[1]),
    ]
    for copy in copies:
        copy.start()
    even = lax.axis_index("y") % 2 == 0
    z = iota((512, 512), 0)
    k = iota((512, 512), 1)
    chooser = ones_where(z == 4 * (k % 128) + k // 128)
    for field, source in enumerate((beta, rhs)):
        copies[field].wait()
        out = dot_exact(source[...].reshape(64, 512), chooser)
        width, start = (C_LOW, B_LOW)[field], (0, C_LOW)[field]
        for q in range(4):
            tiles = [out[8 * x : 8 * x + 8, 128 * q : 128 * q + 128] for x in range(8)]
            for x in range(8):
                own[8 * field + x, q] = tiles[x]
            for d in range(width):
                pair[start + d, q] = jnp.where(even, tiles[7 - d], tiles[d])
                other[start + d, q] = jnp.where(even, tiles[d], tiles[7 - d])


def place_of(field, distance):
    return (0, C_LOW)[field] + distance - 1


def corner_kernel(planes, right, left):
    row = iota((8, 128), 0)
    for t, (field, one, two, rows) in enumerate(CORNERS):
        for q in range(4):
            tile = planes[place_of(field, one), q]
            to_right = to_left = tile
            if two:
                beside = planes[place_of(field, two), q]
                to_right = jnp.where(row >= rows, tile, pltpu.roll(beside, rows, 0))
                to_left = jnp.where(row < 8 - rows, tile, pltpu.roll(beside, 8 - rows, 0))
            right[t, q] = to_right
            left[t, q] = to_left


def down_kernel(own, pair, other, own_left, own_right, left_pair, right_pair, left_other, right_other, packed, x0, b0, fx, fy, fz, dinv, c1, x1, r1, fx1, fy1, fz1, dinv1, diag, first, sums, diag1, first1, b1, parts, *, depth):
    n = lax.axis_index("n")
    even = lax.axis_index("y") % 2 == 0
    keep_left = jnp.where(n > 0, 1.0, 0.0).astype(F32)
    keep_right = jnp.where(n < lax.axis_size("n") - 1, 1.0, 0.0).astype(F32)
    lane = iota((24, 128), 1)
    last, begin = lane == 127, lane == 0

    corner = {}
    for t, (field, one, two, rows) in enumerate(CORNERS):
        corner[field, one] = (t, 0)
        if two:
            corner[field, two] = (t, rows)

    def from_side(side, of_pair, of_other):
        return jnp.where(even, of_other, of_pair) if side == 0 else jnp.where(even, of_pair, of_other)

    def plane(field, p, keep_0, keep_1):
        x = p - 8
        out = []
        for q in range(4):
            if 0 <= x < 8:
                parts = [own_left[8 * field + x, q], own[8 * field + x, q], own_right[8 * field + x, q]]
            else:
                side, distance = (0, -x) if x < 0 else (1, x - 7)
                t, rows = corner[field, distance]
                at = place_of(field, distance)
                parts = [
                    from_side(side, left_pair[t, q], left_other[t, q]),
                    from_side(side, pair[at, q], other[at, q]),
                    from_side(side, right_pair[t, q], right_other[t, q]),
                ]
                if rows:
                    parts[0] = pltpu.roll(parts[0], 8 - rows, 0)
                    parts[2] = pltpu.roll(parts[2], rows, 0)
            out.append(jnp.concatenate([parts[0] * keep_0, parts[1], parts[2] * keep_1] if field == 0 else parts, axis=0))
        return out

    def cells(p):
        return plane(0, p, keep_left, keep_right)

    def source(p):
        return plane(1, p, None, None)

    before, after = cells(1), cells(2)
    for q in range(4):
        fx[1, q] = 0.5 * (before[q] + after[q])

    def faces_0(p):
        c, c_next, b = cells(p), cells(p + 1), source(p)
        gx, gz, gy, d = plane_faces(c, c_next, [fx[p - 1, q] for q in range(4)], 0.5, 1, last, begin)
        for q in range(4):
            fx[p, q], fy[p, q], fz[p, q], diag[p, q] = gx[q], gy[q], gz[q], d[q]
            inv = inverse(c[q], d[q])
            dinv[p, q] = inv
            b0[p, q] = b[q]
            first[p, q] = b[q] * inv * (1.0 / THETA)

    loop(2, 22, faces_0)

    def second_0(p):
        near = neighbours(first, fx, fz, fy, p, 4, 1)
        for q in range(4):
            x0[p, q] = (1.0 + KEEP - GAIN) * first[p, q] + GAIN * (b0[p, q] + near[q]) * dinv[p, q]

    loop(3, 21, second_0)

    def residual_0(k):
        total = [jnp.zeros((24, 128), F32)] * 2
        for p in (4 + 2 * k, 5 + 2 * k):
            near = neighbours(x0, fx, fz, fy, p, 4, 1)
            for q in range(4):
                total[q // 2] = total[q // 2] + (b0[p, q] + near[q] - diag[p, q] * x0[p, q])
        for q in range(2):
            sums[k, q, 0:24] = total[q]
            sums[k, q, 24:32] = jnp.zeros((8, 128), F32)

    loop(0, 8, residual_0)

    def cells_1(k):
        one, two = cells(2 + 2 * k), cells(3 + 2 * k)
        for q in range(2):
            sums[8 + k, q, 0:24] = (one[2 * q] + one[2 * q + 1]) + (two[2 * q] + two[2 * q + 1])
            sums[8 + k, q, 24:32] = jnp.zeros((8, 128), F32)

    loop(0, 10, cells_1)

    def halve(k, q):
        return 0.125 * (sums[k, q, pl.ds(0, 16, stride=2), :] + sums[k, q, pl.ds(1, 16, stride=2), :])

    for q in range(2):
        loop(0, 8, lambda k, q=q: b1.__setitem__((k + 1, q), halve(k, q)))
        loop(0, 10, lambda k, q=q: c1.__setitem__((k, q), halve(8 + k, q)))

    lane = iota((16, 128), 1)
    last_1, begin_1 = lane == 127, lane == 0
    for q in range(2):
        fx1[0, q] = 0.125 * (c1[0, q] + c1[1, q])

    def faces_1(p):
        c, c_next = [c1[p, q] for q in range(2)], [c1[p + 1, q] for q in range(2)]
        gx, gz, gy, d = plane_faces(c, c_next, [fx1[p - 1, q] for q in range(2)], 0.125, 1, last_1, begin_1)
        for q in range(2):
            fx1[p, q], fy1[p, q], fz1[p, q], diag1[p, q] = gx[q], gy[q], gz[q], d[q]
            inv = inverse(c[q], d[q])
            dinv1[p, q] = inv
            first1[p, q] = b1[p, q] * inv * (1.0 / THETA)

    loop(1, 9, faces_1)

    def second_1(p):
        near = neighbours(first1, fx1, fz1, fy1, p, 2, 1)
        for q in range(2):
            x1[p, q] = (1.0 + KEEP - GAIN) * first1[p, q] + GAIN * (b1[p, q] + near[q]) * dinv1[p, q]

    loop(2, 8, second_1)

    y, size = lax.axis_index("y"), lax.axis_size("n")
    for x in range(2):
        total = jnp.zeros((16, 128), F32)
        cell = jnp.zeros((16, 128), F32)
        for p in (3 + 2 * x, 4 + 2 * x):
            near = neighbours(x1, fx1, fz1, fy1, p, 2, 1)
            for q in range(2):
                rest = b1[p, q] + near[q] - diag1[p, q] * x1[p, q]
                r1[p, q] = rest
                total = total + rest
                cell = cell + c1[p, q]
                place = p - 3
                parts[place // 2, place % 2, 4 * q : 4 * q + 4] = rest[4:8]
                row = 4 * (place % 2) + 2 * q
                parts[2, place // 2, row : row + 2] = rest[6:8]
                parts[3, place // 2, row : row + 2] = rest[4:6]
        total = 0.125 * (total + shift(total, 1, 0))
        cell = 0.125 * (cell + shift(cell, 1, 0))
        for yy in range(2):
            packed[0, 2, 2 * x + yy : 2 * x + yy + 1] = total[4 + 2 * yy : 5 + 2 * yy]
            packed[0, 2, 4 + 2 * x + yy : 5 + 2 * x + yy] = cell[4 + 2 * yy : 5 + 2 * yy]

    level_two = packed[0, 2]
    for y_to in range(depth):
        ahead = (y_to - y + depth) % depth
        for n_to in range(size):
            beside = jnp.where(n_to > n, 2, 3)
            part = jnp.where(ahead == 0, beside, jnp.where(ahead == 1, 1, 0))
            s = y_to * size + n_to
            packed[s, 0] = parts[part, 0]
            packed[s, 1] = parts[part, 1]
            packed[s, 2] = level_two


def edge_kernel(plane, other, pair, *, depth):
    n = lax.axis_index("n")
    even = lax.axis_index("z") % 2 == 0
    size = lax.axis_size("n")

    count = (depth - 1) * size
    def send(s, up, down):
        pair[s] = jnp.where(even, up, down)
        other[s] = jnp.where(even, down, up)

    for s in range(count):
        send(s, plane[size + s, 2], plane[s, 2])
    for k in range(3):
        place = jnp.clip(n + (k - 1), 0, size - 1)
        for j in range(2):
            send(count + 2 * k + j, plane[count + place, j], plane[place, j])


def middle_kernel(plane, other, pair, r1, sent, x2, r2, fx, fy, fz, dinv, r1h, b2, c2, diag, first, half, *, depth, tall):
    z, y, n = lax.axis_index("z"), lax.axis_index("y"), lax.axis_index("n")
    size = lax.axis_size("n")
    even = z % 2 == 0

    def below(rows):
        return jnp.where(even, other[rows, :], pair[rows, :])

    def above(rows):
        return jnp.where(even, pair[rows, :], other[rows, :])

    width = 2 * depth
    for yb in range(depth):
        for x in range(2):
            for yy in range(2):
                r = 2 * x + yy
                place = 2 * yb + x
                own = yb * size * 24 + 16 + r
                b2[width + place, yy] = plane[pl.ds(own, 8, stride=24), :]
                c2[width + place, yy] = plane[pl.ds(own + 4, 8, stride=24), :]
                if yb > 0:
                    edge = (yb - 1) * size * 8 + r
                    b2[place, yy] = below(pl.ds(edge, 8, stride=8))
                    c2[place, yy] = below(pl.ds(edge + 4, 8, stride=8))
                if yb < depth - 1:
                    edge = yb * size * 8 + r
                    b2[2 * width + place, yy] = above(pl.ds(edge, 8, stride=8))
                    c2[2 * width + place, yy] = above(pl.ds(edge + 4, 8, stride=8))

    scale = 0.5 / 16.0
    shape = (8, 128)
    row, lane = iota(shape, 0), iota(shape, 1)
    last, begin, last_b, begin_b = row == 7, row == 0, lane == 127, lane == 0
    for q in range(2):
        fx[2, q] = scale * (c2[2, q] + c2[3, q])

    def faces_2(p):
        c, c_next = [c2[p, q] for q in range(2)], [c2[p + 1, q] for q in range(2)]
        gx, gy, gz, d = plane_faces(c, c_next, [fx[p - 1, q] for q in range(2)], scale, 0, last, begin, last_b, begin_b)
        for q in range(2):
            fx[p, q], fy[p, q], fz[p, q], diag[p, q] = gx[q], gy[q], gz[q], d[q]
            inv = inverse(c[q], d[q])
            dinv[p, q] = inv
            first[p, q] = b2[p, q] * inv * (1.0 / THETA)

    loop(3, 3 * width - 3, faces_2)

    def second_2(p):
        near = neighbours(first, fx, fy, fz, p, 2, 0)
        for q in range(2):
            x2[p, q] = (1.0 + KEEP - GAIN) * first[p, q] + GAIN * (b2[p, q] + near[q]) * dinv[p, q]

    loop(4, 3 * width - 4, second_2)

    totals = [jnp.zeros(shape, F32)] * depth
    cell_sums = [jnp.zeros(shape, F32)] * depth
    for p in range(5, 3 * width - 5):
        near = neighbours(x2, fx, fy, fz, p, 2, 0)
        j = (p - width) // 2
        for q in range(2):
            rest = b2[p, q] + near[q] - diag[p, q] * x2[p, q]
            r2[p, q] = rest
            if 0 <= j < depth:
                totals[j] = totals[j] + rest
                cell_sums[j] = cell_sums[j] + c2[p, q]
    zz, k = iota((128, 128), 0), iota((128, 128), 1)
    low_half = ones_where(k == zz // 2, 0.125)
    high_half = ones_where(k == zz // 2 + 64, 0.125)
    coarse = dot_exact(jnp.concatenate(totals, axis=0), low_half) + dot_exact(jnp.concatenate(cell_sums, axis=0), high_half)
    for j in range(depth):
        half[j // 2, j % 2] = coarse[8 * j : 8 * j + 8]
    mine = half[n % 2]
    for s in range(tall):
        sent[s] = mine

    for p in range(3, 7):
        for q in range(2):
            r1h[p, q] = r1[p, q]
    edges = 8 * (depth - 1) * size
    for k in range(3):
        place = jnp.clip(n + (k - 1), 0, size - 1)

        def block(yb, j):
            start = pl.multiple_of((yb * size + place) * 24 + 8 * j, 8)
            return plane[pl.ds(start, 8), :]

        for j in range(2):
            start = edges + 8 * (2 * k + j)
            low = jnp.where(y == 0, below(pl.ds(start, 8)), block(jnp.maximum(y - 1, 0), j))
            high = jnp.where(y == depth - 1, above(pl.ds(start, 8)), block(jnp.minimum(y + 1, depth - 1), j))
            for q in range(2):
                r1h[1 + j, q, 4 * k : 4 * k + 4] = low[4 * q : 4 * q + 4]
                r1h[7 + j, q, 4 * k : 4 * k + 4] = high[4 * q : 4 * q + 4]
                r1h[1 + j, q, 12:16] = jnp.zeros((4, 128), F32)
                r1h[7 + j, q, 12:16] = jnp.zeros((4, 128), F32)
            if k != 1:
                tile = block(y, j)
                start = 2 if k == 0 else 8
                for x in range(2):
                    for q in range(2):
                        row = 4 * x + 2 * q
                        r1h[3 + 2 * j + x, q, start : start + 2] = tile[row : row + 2]


def sweeps(start, mid, out, source, fx, fa, fb, dinv, low, planes, count, axis):
    def one(p):
        near = neighbours(start, fx, fa, fb, p, count, axis)
        for q in range(count):
            mid[p, q] = (1.0 - 1.0 / THETA) * start[p, q] + (1.0 / THETA) * ((source[p, q] + near[q]) * dinv[p, q])

    loop(-1, planes + 1, lambda k: one(low + k))

    def two(p):
        near = neighbours(mid, fx, fa, fb, p, count, axis)
        for q in range(count):
            value = (1.0 - GAIN + KEEP) * mid[p, q] - KEEP * start[p, q]
            out(p, q, value + GAIN * ((source[p, q] + near[q]) * dinv[p, q]))

    loop(0, planes, lambda k: two(low + k))


def up_kernel(gathered, r1h, x2, r2, fx2, fy2, fz2, dinv2, c1, x1, fx1, fy1, fz1, dinv1, x0, b0, fx, fy, fz, dinv, result,
              c3, p3, r3, x3, i3, fx3, fy3, fz3, d3, s2, m2, f2, s1, m1, f1, s0, m0, f0, *, depth, tall):
    z, y, n = lax.axis_index("z"), lax.axis_index("y"), lax.axis_index("n")
    half = depth * tall // 2
    shape = (8, 128)
    row, lane = iota(shape, 0), iota(shape, 1)
    upper = lane >= 64

    def unpack(i):
        one, two = [gathered[j % depth // 2, j // depth, j % 2] for j in (i, i + half)]
        b = jnp.where(upper, pltpu.roll(two, 64, 1), one)
        c3[i + 1, 0] = jnp.where(upper, two, pltpu.roll(one, 64, 1))
        r3[i + 1, 0] = b
        p3[i + 1, 0] = b
        x3[i + 1, 0] = jnp.zeros(shape, F32)

    loop(0, half, unpack)

    def wrap(ref):
        ref[0, 0] = jnp.where(upper, pltpu.roll(ref[half, 0], 64, 1), 0.0)
        ref[half + 1, 0] = jnp.where(upper, 0.0, pltpu.roll(ref[1, 0], 64, 1))

    wrap(c3)
    scale = 0.5 / 64.0
    fx3[0, 0] = scale * (c3[0, 0] + c3[1, 0])

    def faces_3(p):
        gx, gy, gz, d = plane_faces([c3[p, 0]], [c3[p + 1, 0]], [fx3[p - 1, 0]], scale, 0, row == 7, row == 0, lane % 64 == 63, lane % 64 == 0)
        fx3[p, 0], fy3[p, 0], fz3[p, 0], d3[p, 0] = gx[0], gy[0], gz[0], d[0]

    loop(1, half + 1, faces_3)

    def whole(parts):
        total = functools.reduce(lambda a, b: a + b, parts)
        return jnp.sum(jnp.sum(total, axis=0, keepdims=True), axis=1, keepdims=True)

    def spread(values):
        parts = [jnp.zeros(shape, F32)] * 4
        for i, value in enumerate(values):
            parts[i % 4] = parts[i % 4] + value
        return whole(parts)

    start_norm = spread([r3[i + 1, 0] * r3[i + 1, 0] for i in range(half)])

    def iterate(norm):
        wrap(p3)
        products = []
        for p in range(1, half + 1):
            here = p3[p, 0]
            image = d3[p, 0] * here - neighbours(p3, fx3, fy3, fz3, p, 1, 0)[0]
            i3[p, 0] = image
            products.append(here * image)
        alpha = norm / spread(products)
        squares = []
        for p in range(1, half + 1):
            x3[p, 0] = x3[p, 0] + alpha * p3[p, 0]
            rest = r3[p, 0] - alpha * i3[p, 0]
            r3[p, 0] = rest
            squares.append(rest * rest)
        new = spread(squares)
        beta = new / norm
        for p in range(1, half + 1):
            p3[p, 0] = r3[p, 0] + beta * p3[p, 0]
        return new

    norm = start_norm
    for _ in range(COARSE_SWEEPS):
        norm = iterate(norm)

    base = 2 * depth + 2 * y - 4
    tiles = []
    for j in range(5):
        place = jnp.clip(depth * z + y - 2 + j, 0, 2 * half - 1)
        high = place >= half
        tile = x3[jnp.where(high, place - half, place) + 1, 0]
        tiles.append(jnp.where(high, pltpu.roll(tile, 64, 1), tile))
    k, zz = iota((128, 128), 0), iota((128, 128), 1)
    fine = dot_exact(jnp.concatenate(tiles, axis=0), ones_where(k == zz // 2))
    for j in range(5):
        add = fine[8 * j : 8 * j + 8]
        for p in (base + 2 * j, base + 2 * j + 1):
            for q in range(2):
                s2[p, q] = jnp.where(dinv2[p, q] > 0.0, add, 0.0)

    def keep_2(p, q, value):
        f2[p, q] = x2[p, q] + value

    sweeps(s2, m2, keep_2, r2, fx2, fy2, fz2, dinv2, base + 2, 6, 2, 0)

    wide = jnp.concatenate([jnp.concatenate([f2[base + 2 + k, 0], f2[base + 2 + k, 1]], axis=0) for k in range(6)], axis=1)
    r, k = iota((16, 16), 0), iota((16, 16), 1)
    from_n = n + r // 4 - 1
    pick = ones_where((k == (r // 2) % 2 * 8 + from_n) & (from_n >= 0) & (from_n < 8))
    fine = chosen_dot(pick, wide)
    for p in range(10):
        k = (p + 1) // 2
        for q in range(2):
            s1[p, q] = jnp.where(c1[p, q] > 0.0, fine[:, 128 * k : 128 * k + 128], 0.0)

    def keep_1(p, q, value):
        f1[p, q] = x1[p, q] + value

    sweeps(s1, m1, keep_1, r1h, fx1, fz1, fy1, dinv1, 2, 6, 2, 1)

    wide = jnp.concatenate([f1[p, q] for p in range(2, 8) for q in range(2)], axis=1)
    r, k = iota((24, 16), 0), iota((24, 16), 1)
    fine = chosen_dot(ones_where(k == r // 2), wide)
    for p in range(6, 18):
        for q in range(4):
            j = 2 * (p // 2 - 3) + q // 2
            s0[p, q] = jnp.where(dinv[p, q] > 0.0, x0[p, q] + fine[:, 128 * j : 128 * j + 128], 0.0)

    def keep_0(p, q, value):
        start = (p - 8) * 8
        if not isinstance(start, int):
            start = pl.multiple_of(start, 8)
        f0[pl.ds(start, 8), 128 * q : 128 * q + 128] = value[8:16]

    sweeps(s0, m0, keep_0, b0, fx, fz, fy, dinv, 8, 8, 4, 1)
    k, z0 = iota((512, 512), 0), iota((512, 512), 1)
    back = ones_where(z0 == 4 * (k % 128) + k // 128)
    result[...] = dot_exact(f0[...], back).reshape(8, 8, 512)


def call(kernel, outs, *operands, scratch=(), limit=40):
    shapes = [jax.ShapeDtypeStruct(shape, F32) for shape in outs]
    return pl.pallas_call(
        kernel,
        out_shape=shapes,
        in_specs=[pl.BlockSpec(memory_space=pltpu.VMEM)] * len(operands),
        out_specs=[pl.BlockSpec(memory_space=pltpu.VMEM)] * len(outs),
        scratch_shapes=[pltpu.VMEM(shape, F32) for shape in scratch],
        compiler_params=pltpu.CompilerParams(vmem_limit_bytes=limit * 2**20),
    )(*operands)


def split(rhs_field, beta_cells):
    outs = [(16, 4, 8, 128), (SENT, 4, 8, 128), (SENT, 4, 8, 128)]
    return pl.pallas_call(
        split_kernel,
        out_shape=[jax.ShapeDtypeStruct(shape, F32) for shape in outs],
        in_specs=[pl.BlockSpec(memory_space=pltpu.HBM)] * 2,
        out_specs=[pl.BlockSpec(memory_space=pltpu.VMEM)] * 3,
        scratch_shapes=[pltpu.VMEM((8, 8, 512), F32)] * 2 + [pltpu.SemaphoreType.DMA((2,))],
        compiler_params=pltpu.CompilerParams(vmem_limit_bytes=40 * 2**20),
    )(pltpu.with_memory_space_constraint(rhs_field, pltpu.HBM), pltpu.with_memory_space_constraint(beta_cells, pltpu.HBM))


def ring(axis_size, step):
    return [(i, (i + step) % axis_size) for i in range(axis_size)]


def pairs(axis_size):
    return [(i, i ^ 1) for i in range(axis_size)]


def others(axis_size):
    return [(i, ((i + 1) ^ 1) - 1) for i in range(1, axis_size - 1)]


def shards(rhs_field, beta_cells):
    tall, depth, size = lax.axis_size("z"), lax.axis_size("y"), lax.axis_size("n")
    wide, group = tall * depth, depth * size
    own, to_pair, to_other = split(rhs_field, beta_cells)
    own_left = lax.ppermute(own, "n", ring(size, 1))
    own_right = lax.ppermute(own, "n", ring(size, -1))
    other = lax.ppermute(to_other, ("z", "y"), others(wide))
    pair = lax.ppermute(to_pair, ("z", "y"), pairs(wide))
    corners = []
    for planes in (pair, other):
        to_right, to_left = call(corner_kernel, [(len(CORNERS), 4, 8, 128)] * 2, planes)
        corners += [lax.ppermute(to_right, "n", ring(size, 1)), lax.ppermute(to_left, "n", ring(size, -1))]
    fine, coarse = (24, 4, 24, 128), (10, 2, 16, 128)
    outs = call(
        functools.partial(down_kernel, depth=depth),
        [(group, 3, 8, 128)] + [fine] * 6 + [coarse] * 7,
        own, pair, other, own_left, own_right, *corners,
        scratch=[fine, fine, (18, 2, 32, 128), coarse, coarse, coarse, (4, 2, 8, 128)],
    )
    packed, level_zero = outs[0], outs[1:7]
    c1, x1, r1, *faces_1 = outs[7:14]
    plane = lax.all_to_all(packed, ("y", "n"), 0, 0)
    edge = group - size + 6
    to_other, to_pair = call(functools.partial(edge_kernel, depth=depth), [(edge, 8, 128)] * 2, plane)
    other = lax.ppermute(to_other, "z", others(tall))
    pair = lax.ppermute(to_pair, "z", pairs(tall))
    slab = (6 * depth, 2, 8, 128)
    outs = call(
        functools.partial(middle_kernel, depth=depth, tall=tall),
        [(tall, depth // 2, 8, 128)] + [slab] * 6 + [coarse],
        plane.reshape(group * 24, 128), other.reshape(edge * 8, 128), pair.reshape(edge * 8, 128), r1,
        scratch=[slab, slab, slab, slab, (2, depth // 2, 8, 128)],
    )
    sent, level_two, r1h = outs[0], outs[1:7], outs[7]
    gathered = lax.all_to_all(sent, "z", 0, 0)
    cores = [[2 * i, 2 * i + 1] for i in range(size // 2)]
    gathered = lax.all_gather(gathered, "n", axis_index_groups=cores)
    packed_3 = (wide // 2 + 2, 1, 8, 128)
    (result,) = call(
        functools.partial(up_kernel, depth=depth, tall=tall),
        [(8, 8, 512)],
        gathered, r1h, *level_two, c1, x1, *faces_1, *level_zero,
        scratch=[packed_3] * 9 + [slab] * 3 + [coarse] * 3 + [fine] * 2 + [(64, 512)],
    )
    return result


def solution(mesh):
    wide, size = mesh.shape["wide"], mesh.shape["narrow"]
    inner = Mesh(mesh.devices.reshape(wide // 4, 4, size), ("z", "y", "n"))
    spec = P(("z", "y"), "n", None)
    return jax.shard_map(shards, mesh=inner, in_specs=(spec, spec), out_specs=spec, check_vma=False)
```

```python
import functools

import jax
import jax.numpy as jnp
from jax import lax
from jax.experimental import pallas as pl
from jax.experimental.pallas import tpu as pltpu
from jax.sharding import Mesh, PartitionSpec as P

F32 = jnp.float32
BF16 = jnp.bfloat16

THETA = 0.5 * (2.0 + 0.25)
DELTA = 0.5 * (2.0 - 0.25)
SIGMA = THETA / DELTA
RHO_0 = 1.0 / SIGMA
RHO_1 = 1.0 / (2.0 * SIGMA - RHO_0)
KEEP = RHO_1 * RHO_0
GAIN = 2.0 * RHO_1 / DELTA
COARSE_SWEEPS = 8


def dot_exact(values, chooser):
    high = values.astype(BF16)
    rest = values - high.astype(F32)
    middle = rest.astype(BF16)
    low = (rest - middle.astype(F32)).astype(BF16)
    rows = values.shape[0]
    out = jnp.dot(jnp.concatenate([high, middle, low], axis=0), chooser, preferred_element_type=F32)
    return out[:rows] + out[rows : 2 * rows] + out[2 * rows :]


def chosen_dot(chooser, values):
    high = values.astype(BF16)
    rest = values - high.astype(F32)
    middle = rest.astype(BF16)
    low = (rest - middle.astype(F32)).astype(BF16)
    out = jnp.dot(chooser, high, preferred_element_type=F32)
    out = out + jnp.dot(chooser, middle, preferred_element_type=F32)
    return out + jnp.dot(chooser, low, preferred_element_type=F32)


def iota(shape, dim):
    return lax.broadcasted_iota(jnp.int32, shape, dim)


def ones_where(mask, value=1.0):
    return jnp.where(mask, value, 0.0).astype(BF16)


def shift(values, step, axis):
    size = values.shape[axis]
    return pltpu.roll(values, (-step) % size, axis)


def plane_faces(c, c_next, fx_before, scale, axis, last, first, last_b=None, first_b=None):
    count, other = len(c), 1 - axis
    fx = [scale * (c[q] + c_next[q]) for q in range(count)]
    after = [c[q + 1] if q + 1 < count else jnp.where(last, 0.0, shift(c[0], 1, axis)) for q in range(count)]
    fa = [scale * (c[q] + after[q]) for q in range(count)]
    lowest = jnp.where(first, scale * c[0], shift(fa[-1], -1, axis))
    fb, diagonal = [], []
    for q in range(count):
        beside = shift(c[q], 1, other)
        if last_b is not None:
            beside = jnp.where(last_b, 0.0, beside)
        face = scale * (c[q] + beside)
        face_before = shift(face, -1, other)
        if first_b is not None:
            face_before = jnp.where(first_b, scale * c[q], face_before)
        diagonal.append(fx[q] + fx_before[q] + face + face_before + fa[q] + (fa[q - 1] if q else lowest))
        fb.append(face if last_b is None else jnp.where(last_b, 0.0, face))
    fa[-1] = jnp.where(last, 0.0, fa[-1])
    return fx, fa, fb, diagonal


def neighbours(u, fx, fa, fb, p, count, axis):
    other = 1 - axis
    here = [u[p, q] for q in range(count)]
    faces = [fa[p, q] for q in range(count)]
    out = []
    for q in range(count):
        face = fb[p, q]
        total = fx[p, q] * u[p + 1, q] + fx[p - 1, q] * u[p - 1, q]
        total = total + face * shift(here[q], 1, other) + shift(face * here[q], -1, other)
        if q + 1 < count:
            total = total + faces[q] * here[q + 1]
        else:
            total = total + faces[q] * shift(here[0], 1, axis)
        if q > 0:
            total = total + faces[q - 1] * here[q - 1]
        else:
            total = total + shift(faces[-1] * here[-1], -1, axis)
        out.append(total)
    return out


def loop(low, high, body):
    for k in range(high - low):
        body(low + k)


def inverse(c, diagonal):
    return jnp.where(c > 0.0, 1.0 / diagonal, 0.0)


C_LOW, B_LOW = 7, 6
SENT = C_LOW + B_LOW

CORNERS = (
    (0, 1, 0, 0), (0, 2, 0, 0), (0, 3, 7, 2), (0, 4, 6, 3), (0, 5, 0, 0),
    (1, 1, 6, 2), (1, 2, 0, 0), (1, 3, 5, 3), (1, 4, 0, 0),
)


def split_kernel(rhs_hbm, beta_hbm, own, pair, other, rhs, beta, sems):
    copies = [
        pltpu.make_async_copy(beta_hbm, beta, sems.at[0]),
        pltpu.make_async_copy(rhs_hbm, rhs, sems.at[1]),
    ]
    for copy in copies:
        copy.start()
    even = lax.axis_index("y") % 2 == 0
    z = iota((512, 512), 0)
    k = iota((512, 512), 1)
    chooser = ones_where(z == 4 * (k % 128) + k // 128)
    for field, source in enumerate((beta, rhs)):
        copies[field].wait()
        out = dot_exact(source[...].reshape(64, 512), chooser)
        width, start = (C_LOW, B_LOW)[field], (0, C_LOW)[field]
        for q in range(4):
            tiles = [out[8 * x : 8 * x + 8, 128 * q : 128 * q + 128] for x in range(8)]
            for x in range(8):
                own[8 * field + x, q] = tiles[x]
            for d in range(width):
                pair[start + d, q] = jnp.where(even, tiles[7 - d], tiles[d])
                other[start + d, q] = jnp.where(even, tiles[d], tiles[7 - d])


def place_of(field, distance):
    return (0, C_LOW)[field] + distance - 1


def corner_kernel(planes, right, left):
    row = iota((8, 128), 0)
    for t, (field, one, two, rows) in enumerate(CORNERS):
        for q in range(4):
            tile = planes[place_of(field, one), q]
            to_right = to_left = tile
            if two:
                beside = planes[place_of(field, two), q]
                to_right = jnp.where(row >= rows, tile, pltpu.roll(beside, rows, 0))
                to_left = jnp.where(row < 8 - rows, tile, pltpu.roll(beside, 8 - rows, 0))
            right[t, q] = to_right
            left[t, q] = to_left


def down_kernel(own, pair, other, own_left, own_right, left_pair, right_pair, left_other, right_other, packed, x0, b0, fx, fy, fz, dinv, c1, x1, r1, fx1, fy1, fz1, dinv1, diag, first, sums, diag1, first1, b1, parts, *, depth):
    n = lax.axis_index("n")
    even = lax.axis_index("y") % 2 == 0
    keep_left = jnp.where(n > 0, 1.0, 0.0).astype(F32)
    keep_right = jnp.where(n < lax.axis_size("n") - 1, 1.0, 0.0).astype(F32)
    lane = iota((24, 128), 1)
    last, begin = lane == 127, lane == 0

    corner = {}
    for t, (field, one, two, rows) in enumerate(CORNERS):
        corner[field, one] = (t, 0)
        if two:
            corner[field, two] = (t, rows)

    def from_side(side, of_pair, of_other):
        return jnp.where(even, of_other, of_pair) if side == 0 else jnp.where(even, of_pair, of_other)

    def plane(field, p, keep_0, keep_1):
        x = p - 8
        out = []
        for q in range(4):
            if 0 <= x < 8:
                parts = [own_left[8 * field + x, q], own[8 * field + x, q], own_right[8 * field + x, q]]
            else:
                side, distance = (0, -x) if x < 0 else (1, x - 7)
                t, rows = corner[field, distance]
                at = place_of(field, distance)
                parts = [
                    from_side(side, left_pair[t, q], left_other[t, q]),
                    from_side(side, pair[at, q], other[at, q]),
                    from_side(side, right_pair[t, q], right_other[t, q]),
                ]
                if rows:
                    parts[0] = pltpu.roll(parts[0], 8 - rows, 0)
                    parts[2] = pltpu.roll(parts[2], rows, 0)
            out.append(jnp.concatenate([parts[0] * keep_0, parts[1], parts[2] * keep_1] if field == 0 else parts, axis=0))
        return out

    planes = {}

    def cells(p):
        if p not in planes:
            planes[p] = plane(0, p, keep_left, keep_right)
        return planes[p]

    def source(p):
        return plane(1, p, None, None)

    before, after = cells(1), cells(2)
    for q in range(4):
        fx[1, q] = 0.5 * (before[q] + after[q])

    def cells_1(k):
        one, two = cells(2 + 2 * k), cells(3 + 2 * k)
        for q in range(2):
            sums[8 + k, q, 0:24] = (one[2 * q] + one[2 * q + 1]) + (two[2 * q] + two[2 * q + 1])
            sums[8 + k, q, 24:32] = jnp.zeros((8, 128), F32)

    def faces_0(p):
        c, c_next, b = cells(p), cells(p + 1), source(p)
        if p % 2:
            cells_1((p - 3) // 2)
        gx, gz, gy, d = plane_faces(c, c_next, [fx[p - 1, q] for q in range(4)], 0.5, 1, last, begin)
        for q in range(4):
            fx[p, q], fy[p, q], fz[p, q], diag[p, q] = gx[q], gy[q], gz[q], d[q]
            inv = inverse(c[q], d[q])
            dinv[p, q] = inv
            b0[p, q] = b[q]
            first[p, q] = b[q] * inv * (1.0 / THETA)

    loop(2, 22, faces_0)

    def second_0(p):
        near = neighbours(first, fx, fz, fy, p, 4, 1)
        for q in range(4):
            x0[p, q] = (1.0 + KEEP - GAIN) * first[p, q] + GAIN * (b0[p, q] + near[q]) * dinv[p, q]

    loop(3, 21, second_0)

    def residual_0(k):
        total = [jnp.zeros((24, 128), F32)] * 2
        for p in (4 + 2 * k, 5 + 2 * k):
            near = neighbours(x0, fx, fz, fy, p, 4, 1)
            for q in range(4):
                total[q // 2] = total[q // 2] + (b0[p, q] + near[q] - diag[p, q] * x0[p, q])
        for q in range(2):
            sums[k, q, 0:24] = total[q]
            sums[k, q, 24:32] = jnp.zeros((8, 128), F32)

    loop(0, 8, residual_0)

    def halve(k, q):
        return 0.125 * (sums[k, q, pl.ds(0, 16, stride=2), :] + sums[k, q, pl.ds(1, 16, stride=2), :])

    for q in range(2):
        loop(0, 8, lambda k, q=q: b1.__setitem__((k + 1, q), halve(k, q)))
        loop(0, 10, lambda k, q=q: c1.__setitem__((k, q), halve(8 + k, q)))

    lane = iota((16, 128), 1)
    last_1, begin_1 = lane == 127, lane == 0
    for q in range(2):
        fx1[0, q] = 0.125 * (c1[0, q] + c1[1, q])

    def faces_1(p):
        c, c_next = [c1[p, q] for q in range(2)], [c1[p + 1, q] for q in range(2)]
        gx, gz, gy, d = plane_faces(c, c_next, [fx1[p - 1, q] for q in range(2)], 0.125, 1, last_1, begin_1)
        for q in range(2):
            fx1[p, q], fy1[p, q], fz1[p, q], diag1[p, q] = gx[q], gy[q], gz[q], d[q]
            inv = inverse(c[q], d[q])
            dinv1[p, q] = inv
            first1[p, q] = b1[p, q] * inv * (1.0 / THETA)

    loop(1, 9, faces_1)

    def second_1(p):
        near = neighbours(first1, fx1, fz1, fy1, p, 2, 1)
        for q in range(2):
            x1[p, q] = (1.0 + KEEP - GAIN) * first1[p, q] + GAIN * (b1[p, q] + near[q]) * dinv1[p, q]

    loop(2, 8, second_1)

    y, size = lax.axis_index("y"), lax.axis_size("n")
    for x in range(2):
        total = jnp.zeros((16, 128), F32)
        cell = jnp.zeros((16, 128), F32)
        for p in (3 + 2 * x, 4 + 2 * x):
            near = neighbours(x1, fx1, fz1, fy1, p, 2, 1)
            for q in range(2):
                rest = b1[p, q] + near[q] - diag1[p, q] * x1[p, q]
                r1[p, q] = rest
                total = total + rest
                cell = cell + c1[p, q]
                place = p - 3
                parts[place // 2, place % 2, 4 * q : 4 * q + 4] = rest[4:8]
                row = 4 * (place % 2) + 2 * q
                parts[2, place // 2, row : row + 2] = rest[6:8]
                parts[3, place // 2, row : row + 2] = rest[4:6]
        total = 0.125 * (total + shift(total, 1, 0))
        cell = 0.125 * (cell + shift(cell, 1, 0))
        for yy in range(2):
            packed[0, 2, 2 * x + yy : 2 * x + yy + 1] = total[4 + 2 * yy : 5 + 2 * yy]
            packed[0, 2, 4 + 2 * x + yy : 5 + 2 * x + yy] = cell[4 + 2 * yy : 5 + 2 * yy]

    level_two = packed[0, 2]
    for y_to in range(depth):
        ahead = (y_to - y + depth) % depth
        for n_to in range(size):
            beside = jnp.where(n_to > n, 2, 3)
            part = jnp.where(ahead == 0, beside, jnp.where(ahead == 1, 1, 0))
            s = y_to * size + n_to
            packed[s, 0] = parts[part, 0]
            packed[s, 1] = parts[part, 1]
            packed[s, 2] = level_two


def edge_kernel(plane, other, pair, *, depth):
    n = lax.axis_index("n")
    even = lax.axis_index("z") % 2 == 0
    size = lax.axis_size("n")

    count = (depth - 1) * size
    def send(s, up, down):
        pair[s] = jnp.where(even, up, down)
        other[s] = jnp.where(even, down, up)

    for s in range(count):
        send(s, plane[size + s, 2], plane[s, 2])
    for k in range(3):
        place = jnp.clip(n + (k - 1), 0, size - 1)
        for j in range(2):
            send(count + 2 * k + j, plane[count + place, j], plane[place, j])


def middle_kernel(plane, other, pair, r1, sent, x2, r2, fx, fy, fz, dinv, r1h, b2, c2, diag, first, half, *, depth, tall):
    z, y, n = lax.axis_index("z"), lax.axis_index("y"), lax.axis_index("n")
    size = lax.axis_size("n")
    even = z % 2 == 0

    def below(rows):
        return jnp.where(even, other[rows, :], pair[rows, :])

    def above(rows):
        return jnp.where(even, pair[rows, :], other[rows, :])

    width = 2 * depth
    for yb in range(depth):
        for x in range(2):
            for yy in range(2):
                r = 2 * x + yy
                place = 2 * yb + x
                own = yb * size * 24 + 16 + r
                b2[width + place, yy] = plane[pl.ds(own, 8, stride=24), :]
                c2[width + place, yy] = plane[pl.ds(own + 4, 8, stride=24), :]
                if yb > 0:
                    edge = (yb - 1) * size * 8 + r
                    b2[place, yy] = below(pl.ds(edge, 8, stride=8))
                    c2[place, yy] = below(pl.ds(edge + 4, 8, stride=8))
                if yb < depth - 1:
                    edge = yb * size * 8 + r
                    b2[2 * width + place, yy] = above(pl.ds(edge, 8, stride=8))
                    c2[2 * width + place, yy] = above(pl.ds(edge + 4, 8, stride=8))

    scale = 0.5 / 16.0
    shape = (8, 128)
    row, lane = iota(shape, 0), iota(shape, 1)
    last, begin, last_b, begin_b = row == 7, row == 0, lane == 127, lane == 0
    for q in range(2):
        fx[2, q] = scale * (c2[2, q] + c2[3, q])

    def faces_2(p):
        c, c_next = [c2[p, q] for q in range(2)], [c2[p + 1, q] for q in range(2)]
        gx, gy, gz, d = plane_faces(c, c_next, [fx[p - 1, q] for q in range(2)], scale, 0, last, begin, last_b, begin_b)
        for q in range(2):
            fx[p, q], fy[p, q], fz[p, q], diag[p, q] = gx[q], gy[q], gz[q], d[q]
            inv = inverse(c[q], d[q])
            dinv[p, q] = inv
            first[p, q] = b2[p, q] * inv * (1.0 / THETA)

    loop(3, 3 * width - 3, faces_2)

    def second_2(p):
        near = neighbours(first, fx, fy, fz, p, 2, 0)
        for q in range(2):
            x2[p, q] = (1.0 + KEEP - GAIN) * first[p, q] + GAIN * (b2[p, q] + near[q]) * dinv[p, q]

    loop(4, 3 * width - 4, second_2)

    totals = [jnp.zeros(shape, F32)] * depth
    cell_sums = [jnp.zeros(shape, F32)] * depth
    for p in range(5, 3 * width - 5):
        near = neighbours(x2, fx, fy, fz, p, 2, 0)
        j = (p - width) // 2
        for q in range(2):
            rest = b2[p, q] + near[q] - diag[p, q] * x2[p, q]
            r2[p, q] = rest
            if 0 <= j < depth:
                totals[j] = totals[j] + rest
                cell_sums[j] = cell_sums[j] + c2[p, q]
    zz, k = iota((128, 128), 0), iota((128, 128), 1)
    low_half = ones_where(k == zz // 2, 0.125)
    high_half = ones_where(k == zz // 2 + 64, 0.125)
    coarse = dot_exact(jnp.concatenate(totals, axis=0), low_half) + dot_exact(jnp.concatenate(cell_sums, axis=0), high_half)
    for j in range(depth):
        half[j // 2, j % 2] = coarse[8 * j : 8 * j + 8]
    mine = half[n % 2]
    for s in range(tall):
        sent[s] = mine

    for p in range(3, 7):
        for q in range(2):
            r1h[p, q] = r1[p, q]
    edges = 8 * (depth - 1) * size
    for k in range(3):
        place = jnp.clip(n + (k - 1), 0, size - 1)

        def block(yb, j):
            start = pl.multiple_of((yb * size + place) * 24 + 8 * j, 8)
            return plane[pl.ds(start, 8), :]

        for j in range(2):
            start = edges + 8 * (2 * k + j)
            low = jnp.where(y == 0, below(pl.ds(start, 8)), block(jnp.maximum(y - 1, 0), j))
            high = jnp.where(y == depth - 1, above(pl.ds(start, 8)), block(jnp.minimum(y + 1, depth - 1), j))
            for q in range(2):
                r1h[1 + j, q, 4 * k : 4 * k + 4] = low[4 * q : 4 * q + 4]
                r1h[7 + j, q, 4 * k : 4 * k + 4] = high[4 * q : 4 * q + 4]
                r1h[1 + j, q, 12:16] = jnp.zeros((4, 128), F32)
                r1h[7 + j, q, 12:16] = jnp.zeros((4, 128), F32)
            if k != 1:
                tile = block(y, j)
                start = 2 if k == 0 else 8
                for x in range(2):
                    for q in range(2):
                        row = 4 * x + 2 * q
                        r1h[3 + 2 * j + x, q, start : start + 2] = tile[row : row + 2]


def sweeps(start, mid, out, source, fx, fa, fb, dinv, low, planes, count, axis):
    def one(p):
        near = neighbours(start, fx, fa, fb, p, count, axis)
        for q in range(count):
            mid[p, q] = (1.0 - 1.0 / THETA) * start[p, q] + (1.0 / THETA) * ((source[p, q] + near[q]) * dinv[p, q])

    loop(-1, planes + 1, lambda k: one(low + k))

    def two(p):
        near = neighbours(mid, fx, fa, fb, p, count, axis)
        for q in range(count):
            value = (1.0 - GAIN + KEEP) * mid[p, q] - KEEP * start[p, q]
            out(p, q, value + GAIN * ((source[p, q] + near[q]) * dinv[p, q]))

    loop(0, planes, lambda k: two(low + k))


def up_kernel(gathered, r1h, x2, r2, fx2, fy2, fz2, dinv2, c1, x1, fx1, fy1, fz1, dinv1, x0, b0, fx, fy, fz, dinv, result,
              c3, p3, r3, x3, i3, fx3, fy3, fz3, d3, s2, m2, f2, s1, m1, f1, s0, m0, f0, *, depth, tall):
    z, y, n = lax.axis_index("z"), lax.axis_index("y"), lax.axis_index("n")
    half = depth * tall // 2
    shape = (8, 128)
    row, lane = iota(shape, 0), iota(shape, 1)
    upper = lane >= 64

    def unpack(i):
        one, two = [gathered[j % depth // 2, j // depth, j % 2] for j in (i, i + half)]
        b = jnp.where(upper, pltpu.roll(two, 64, 1), one)
        c3[i + 1, 0] = jnp.where(upper, two, pltpu.roll(one, 64, 1))
        r3[i + 1, 0] = b
        p3[i + 1, 0] = b
        x3[i + 1, 0] = jnp.zeros(shape, F32)

    loop(0, half, unpack)

    def wrap(ref):
        ref[0, 0] = jnp.where(upper, pltpu.roll(ref[half, 0], 64, 1), 0.0)
        ref[half + 1, 0] = jnp.where(upper, 0.0, pltpu.roll(ref[1, 0], 64, 1))

    wrap(c3)
    scale = 0.5 / 64.0
    fx3[0, 0] = scale * (c3[0, 0] + c3[1, 0])

    def faces_3(p):
        gx, gy, gz, d = plane_faces([c3[p, 0]], [c3[p + 1, 0]], [fx3[p - 1, 0]], scale, 0, row == 7, row == 0, lane % 64 == 63, lane % 64 == 0)
        fx3[p, 0], fy3[p, 0], fz3[p, 0], d3[p, 0] = gx[0], gy[0], gz[0], d[0]

    loop(1, half + 1, faces_3)

    def whole(parts):
        total = functools.reduce(lambda a, b: a + b, parts)
        return jnp.sum(jnp.sum(total, axis=0, keepdims=True), axis=1, keepdims=True)

    def spread(values):
        parts = [jnp.zeros(shape, F32)] * 4
        for i, value in enumerate(values):
            parts[i % 4] = parts[i % 4] + value
        return whole(parts)

    start_norm = spread([r3[i + 1, 0] * r3[i + 1, 0] for i in range(half)])

    def iterate(norm):
        wrap(p3)
        products = []
        for p in range(1, half + 1):
            here = p3[p, 0]
            image = d3[p, 0] * here - neighbours(p3, fx3, fy3, fz3, p, 1, 0)[0]
            i3[p, 0] = image
            products.append(here * image)
        alpha = norm / spread(products)
        squares = []
        for p in range(1, half + 1):
            x3[p, 0] = x3[p, 0] + alpha * p3[p, 0]
            rest = r3[p, 0] - alpha * i3[p, 0]
            r3[p, 0] = rest
            squares.append(rest * rest)
        new = spread(squares)
        beta = new / norm
        for p in range(1, half + 1):
            p3[p, 0] = r3[p, 0] + beta * p3[p, 0]
        return new

    norm = start_norm
    for _ in range(COARSE_SWEEPS):
        norm = iterate(norm)

    base = 2 * depth + 2 * y - 4
    tiles = []
    for j in range(5):
        place = jnp.clip(depth * z + y - 2 + j, 0, 2 * half - 1)
        high = place >= half
        tile = x3[jnp.where(high, place - half, place) + 1, 0]
        tiles.append(jnp.where(high, pltpu.roll(tile, 64, 1), tile))
    k, zz = iota((128, 128), 0), iota((128, 128), 1)
    fine = dot_exact(jnp.concatenate(tiles, axis=0), ones_where(k == zz // 2))
    for j in range(5):
        add = fine[8 * j : 8 * j + 8]
        for p in (base + 2 * j, base + 2 * j + 1):
            for q in range(2):
                s2[p, q] = jnp.where(dinv2[p, q] > 0.0, add, 0.0)

    def keep_2(p, q, value):
        f2[p, q] = x2[p, q] + value

    sweeps(s2, m2, keep_2, r2, fx2, fy2, fz2, dinv2, base + 2, 6, 2, 0)

    wide = jnp.concatenate([jnp.concatenate([f2[base + 2 + k, 0], f2[base + 2 + k, 1]], axis=0) for k in range(6)], axis=1)
    r, k = iota((16, 16), 0), iota((16, 16), 1)
    from_n = n + r // 4 - 1
    pick = ones_where((k == (r // 2) % 2 * 8 + from_n) & (from_n >= 0) & (from_n < 8))
    fine = chosen_dot(pick, wide)
    for p in range(10):
        k = (p + 1) // 2
        for q in range(2):
            s1[p, q] = jnp.where(c1[p, q] > 0.0, fine[:, 128 * k : 128 * k + 128], 0.0)

    def keep_1(p, q, value):
        f1[p, q] = x1[p, q] + value

    sweeps(s1, m1, keep_1, r1h, fx1, fz1, fy1, dinv1, 2, 6, 2, 1)

    wide = jnp.concatenate([f1[p, q] for p in range(2, 8) for q in range(2)], axis=1)
    r, k = iota((24, 16), 0), iota((24, 16), 1)
    fine = chosen_dot(ones_where(k == r // 2), wide)
    for p in range(6, 18):
        for q in range(4):
            j = 2 * (p // 2 - 3) + q // 2
            s0[p, q] = jnp.where(dinv[p, q] > 0.0, x0[p, q] + fine[:, 128 * j : 128 * j + 128], 0.0)

    def keep_0(p, q, value):
        start = (p - 8) * 8
        if not isinstance(start, int):
            start = pl.multiple_of(start, 8)
        f0[pl.ds(start, 8), 128 * q : 128 * q + 128] = value[8:16]

    sweeps(s0, m0, keep_0, b0, fx, fz, fy, dinv, 8, 8, 4, 1)
    k, z0 = iota((512, 512), 0), iota((512, 512), 1)
    back = ones_where(z0 == 4 * (k % 128) + k // 128)
    result[...] = dot_exact(f0[...], back).reshape(8, 8, 512)


def call(kernel, outs, *operands, scratch=(), limit=40):
    shapes = [jax.ShapeDtypeStruct(shape, F32) for shape in outs]
    return pl.pallas_call(
        kernel,
        out_shape=shapes,
        in_specs=[pl.BlockSpec(memory_space=pltpu.VMEM)] * len(operands),
        out_specs=[pl.BlockSpec(memory_space=pltpu.VMEM)] * len(outs),
        scratch_shapes=[pltpu.VMEM(shape, F32) for shape in scratch],
        compiler_params=pltpu.CompilerParams(vmem_limit_bytes=limit * 2**20),
    )(*operands)


def split(rhs_field, beta_cells):
    outs = [(16, 4, 8, 128), (SENT, 4, 8, 128), (SENT, 4, 8, 128)]
    return pl.pallas_call(
        split_kernel,
        out_shape=[jax.ShapeDtypeStruct(shape, F32) for shape in outs],
        in_specs=[pl.BlockSpec(memory_space=pltpu.HBM)] * 2,
        out_specs=[pl.BlockSpec(memory_space=pltpu.VMEM)] * 3,
        scratch_shapes=[pltpu.VMEM((8, 8, 512), F32)] * 2 + [pltpu.SemaphoreType.DMA((2,))],
        compiler_params=pltpu.CompilerParams(vmem_limit_bytes=40 * 2**20),
    )(pltpu.with_memory_space_constraint(rhs_field, pltpu.HBM), pltpu.with_memory_space_constraint(beta_cells, pltpu.HBM))


def ring(axis_size, step):
    return [(i, (i + step) % axis_size) for i in range(axis_size)]


def pairs(axis_size):
    return [(i, i ^ 1) for i in range(axis_size)]


def others(axis_size):
    return [(i, ((i + 1) ^ 1) - 1) for i in range(1, axis_size - 1)]


def shards(rhs_field, beta_cells):
    tall, depth, size = lax.axis_size("z"), lax.axis_size("y"), lax.axis_size("n")
    wide, group = tall * depth, depth * size
    own, to_pair, to_other = split(rhs_field, beta_cells)
    own_left = lax.ppermute(own, "n", ring(size, 1))
    own_right = lax.ppermute(own, "n", ring(size, -1))
    other = lax.ppermute(to_other, ("z", "y"), others(wide))
    pair = lax.ppermute(to_pair, ("z", "y"), pairs(wide))
    corners = []
    for planes in (pair, other):
        to_right, to_left = call(corner_kernel, [(len(CORNERS), 4, 8, 128)] * 2, planes)
        corners += [lax.ppermute(to_right, "n", ring(size, 1)), lax.ppermute(to_left, "n", ring(size, -1))]
    fine, coarse = (24, 4, 24, 128), (10, 2, 16, 128)
    outs = call(
        functools.partial(down_kernel, depth=depth),
        [(group, 3, 8, 128)] + [fine] * 6 + [coarse] * 7,
        own, pair, other, own_left, own_right, *corners,
        scratch=[fine, fine, (18, 2, 32, 128), coarse, coarse, coarse, (4, 2, 8, 128)],
    )
    packed, level_zero = outs[0], outs[1:7]
    c1, x1, r1, *faces_1 = outs[7:14]
    plane = lax.all_to_all(packed, ("y", "n"), 0, 0)
    edge = group - size + 6
    to_other, to_pair = call(functools.partial(edge_kernel, depth=depth), [(edge, 8, 128)] * 2, plane)
    other = lax.ppermute(to_other, "z", others(tall))
    pair = lax.ppermute(to_pair, "z", pairs(tall))
    slab = (6 * depth, 2, 8, 128)
    outs = call(
        functools.partial(middle_kernel, depth=depth, tall=tall),
        [(tall, depth // 2, 8, 128)] + [slab] * 6 + [coarse],
        plane.reshape(group * 24, 128), other.reshape(edge * 8, 128), pair.reshape(edge * 8, 128), r1,
        scratch=[slab, slab, slab, slab, (2, depth // 2, 8, 128)],
    )
    sent, level_two, r1h = outs[0], outs[1:7], outs[7]
    gathered = lax.all_to_all(sent, "z", 0, 0)
    cores = [[2 * i, 2 * i + 1] for i in range(size // 2)]
    gathered = lax.all_gather(gathered, "n", axis_index_groups=cores)
    packed_3 = (wide // 2 + 2, 1, 8, 128)
    (result,) = call(
        functools.partial(up_kernel, depth=depth, tall=tall),
        [(8, 8, 512)],
        gathered, r1h, *level_two, c1, x1, *faces_1, *level_zero,
        scratch=[packed_3] * 9 + [slab] * 3 + [coarse] * 3 + [fine] * 2 + [(64, 512)],
    )
    return result


def solution(mesh):
    wide, size = mesh.shape["wide"], mesh.shape["narrow"]
    inner = Mesh(mesh.devices.reshape(wide // 4, 4, size), ("z", "y", "n"))
    spec = P(("z", "y"), "n", None)
    return jax.shard_map(shards, mesh=inner, in_specs=(spec, spec), out_specs=spec, check_vma=False)
```

```python
import functools

import jax
import jax.numpy as jnp
from jax import lax
from jax.experimental import pallas as pl
from jax.experimental.pallas import tpu as pltpu
from jax.sharding import Mesh, PartitionSpec as P

F32 = jnp.float32
BF16 = jnp.bfloat16

THETA = 0.5 * (2.0 + 0.25)
DELTA = 0.5 * (2.0 - 0.25)
SIGMA = THETA / DELTA
RHO_0 = 1.0 / SIGMA
RHO_1 = 1.0 / (2.0 * SIGMA - RHO_0)
KEEP = RHO_1 * RHO_0
GAIN = 2.0 * RHO_1 / DELTA
COARSE_SWEEPS = 8


def dot_exact(values, chooser):
    high = values.astype(BF16)
    rest = values - high.astype(F32)
    middle = rest.astype(BF16)
    low = (rest - middle.astype(F32)).astype(BF16)
    rows = values.shape[0]
    out = jnp.dot(jnp.concatenate([high, middle, low], axis=0), chooser, preferred_element_type=F32)
    return out[:rows] + out[rows : 2 * rows] + out[2 * rows :]


def chosen_dot(chooser, values):
    high = values.astype(BF16)
    rest = values - high.astype(F32)
    middle = rest.astype(BF16)
    low = (rest - middle.astype(F32)).astype(BF16)
    out = jnp.dot(chooser, high, preferred_element_type=F32)
    out = out + jnp.dot(chooser, middle, preferred_element_type=F32)
    return out + jnp.dot(chooser, low, preferred_element_type=F32)


def iota(shape, dim):
    return lax.broadcasted_iota(jnp.int32, shape, dim)


def ones_where(mask, value=1.0):
    return jnp.where(mask, value, 0.0).astype(BF16)


def shift(values, step, axis):
    size = values.shape[axis]
    return pltpu.roll(values, (-step) % size, axis)


def plane_faces(c, c_next, fx_before, scale, axis, last, first, last_b=None, first_b=None):
    count, other = len(c), 1 - axis
    fx = [scale * (c[q] + c_next[q]) for q in range(count)]
    after = [c[q + 1] if q + 1 < count else jnp.where(last, 0.0, shift(c[0], 1, axis)) for q in range(count)]
    fa = [scale * (c[q] + after[q]) for q in range(count)]
    lowest = jnp.where(first, scale * c[0], shift(fa[-1], -1, axis))
    fb, diagonal = [], []
    for q in range(count):
        beside = shift(c[q], 1, other)
        if last_b is not None:
            beside = jnp.where(last_b, 0.0, beside)
        face = scale * (c[q] + beside)
        face_before = shift(face, -1, other)
        if first_b is not None:
            face_before = jnp.where(first_b, scale * c[q], face_before)
        diagonal.append(fx[q] + fx_before[q] + face + face_before + fa[q] + (fa[q - 1] if q else lowest))
        fb.append(face if last_b is None else jnp.where(last_b, 0.0, face))
    fa[-1] = jnp.where(last, 0.0, fa[-1])
    return fx, fa, fb, diagonal


def neighbours(u, fx, fa, fb, p, count, axis):
    other = 1 - axis
    here = [u[p, q] for q in range(count)]
    faces = [fa[p, q] for q in range(count)]
    out = []
    for q in range(count):
        face = fb[p, q]
        total = fx[p, q] * u[p + 1, q] + fx[p - 1, q] * u[p - 1, q]
        total = total + face * shift(here[q], 1, other) + shift(face * here[q], -1, other)
        if q + 1 < count:
            total = total + faces[q] * here[q + 1]
        else:
            total = total + faces[q] * shift(here[0], 1, axis)
        if q > 0:
            total = total + faces[q - 1] * here[q - 1]
        else:
            total = total + shift(faces[-1] * here[-1], -1, axis)
        out.append(total)
    return out


def loop(low, high, body):
    for k in range(high - low):
        body(low + k)


def inverse(c, diagonal):
    return jnp.where(c > 0.0, 1.0 / diagonal, 0.0)


C_LOW, B_LOW = 7, 6
SENT = C_LOW + B_LOW

CORNERS = (
    (0, 1, 0, 0, 0), (0, 2, 0, 0, 0), (0, 3, 0, 7, 2), (0, 4, 0, 6, 3), (0, 5, 1, 4, 4),
    (1, 1, 1, 6, 2), (1, 2, 0, 0, 0), (1, 3, 1, 5, 3),
)


def split_kernel(rhs_hbm, beta_hbm, own, pair, other, rhs, beta, sems):
    copies = [
        pltpu.make_async_copy(beta_hbm, beta, sems.at[0]),
        pltpu.make_async_copy(rhs_hbm, rhs, sems.at[1]),
    ]
    for copy in copies:
        copy.start()
    even = lax.axis_index("y") % 2 == 0
    z = iota((512, 512), 0)
    k = iota((512, 512), 1)
    chooser = ones_where(z == 4 * (k % 128) + k // 128)
    for field, source in enumerate((beta, rhs)):
        copies[field].wait()
        out = dot_exact(source[...].reshape(64, 512), chooser)
        width, start = (C_LOW, B_LOW)[field], (0, C_LOW)[field]
        for q in range(4):
            tiles = [out[8 * x : 8 * x + 8, 128 * q : 128 * q + 128] for x in range(8)]
            for x in range(8):
                own[8 * field + x, q] = tiles[x]
            for d in range(width):
                pair[start + d, q] = jnp.where(even, tiles[7 - d], tiles[d])
                other[start + d, q] = jnp.where(even, tiles[d], tiles[7 - d])


def place_of(field, distance):
    return (0, C_LOW)[field] + distance - 1


def corner_kernel(planes, right, left):
    row = iota((8, 128), 0)
    for t, (field, one, field_two, two, rows) in enumerate(CORNERS):
        for q in range(4):
            tile = planes[place_of(field, one), q]
            to_right = to_left = tile
            if two:
                beside = planes[place_of(field_two, two), q]
                to_right = jnp.where(row >= rows, tile, pltpu.roll(beside, rows, 0))
                to_left = jnp.where(row < 8 - rows, tile, pltpu.roll(beside, 8 - rows, 0))
            right[t, q] = to_right
            left[t, q] = to_left


def down_kernel(own, pair, other, own_left, own_right, left_pair, right_pair, left_other, right_other, packed, x0, b0, fx, fy, fz, dinv, c1, x1, r1, fx1, fy1, fz1, dinv1, diag, first, sums, diag1, first1, b1, parts, *, depth):
    n = lax.axis_index("n")
    even = lax.axis_index("y") % 2 == 0
    keep_left = jnp.where(n > 0, 1.0, 0.0).astype(F32)
    keep_right = jnp.where(n < lax.axis_size("n") - 1, 1.0, 0.0).astype(F32)
    lane = iota((24, 128), 1)
    last, begin = lane == 127, lane == 0

    corner = {}
    for t, (field, one, field_two, two, rows) in enumerate(CORNERS):
        corner[field, one] = (t, 0)
        if two:
            corner[field_two, two] = (t, rows)
    tile_row = iota((8, 128), 0)

    def from_side(side, of_pair, of_other):
        return jnp.where(even, of_other, of_pair) if side == 0 else jnp.where(even, of_pair, of_other)

    def plane(field, p, keep_0, keep_1):
        x = p - 8
        out = []
        for q in range(4):
            if 0 <= x < 8:
                parts = [own_left[8 * field + x, q], own[8 * field + x, q], own_right[8 * field + x, q]]
            else:
                side, distance = (0, -x) if x < 0 else (1, x - 7)
                t, rows = corner[field, distance]
                at = place_of(field, distance)
                parts = [
                    from_side(side, left_pair[t, q], left_other[t, q]),
                    from_side(side, pair[at, q], other[at, q]),
                    from_side(side, right_pair[t, q], right_other[t, q]),
                ]
                if (field, distance) == (0, 5):
                    parts[0] = jnp.where(tile_row >= 4, parts[0], 0.0)
                    parts[2] = jnp.where(tile_row < 4, parts[2], 0.0)
                if rows:
                    parts[0] = pltpu.roll(parts[0], 8 - rows, 0)
                    parts[2] = pltpu.roll(parts[2], rows, 0)
            out.append(jnp.concatenate([parts[0] * keep_0, parts[1], parts[2] * keep_1] if field == 0 else parts, axis=0))
        return out

    planes = {}

    def cells(p):
        if p not in planes:
            planes[p] = plane(0, p, keep_left, keep_right)
        return planes[p]

    def source(p):
        return plane(1, p, None, None)

    before, after = cells(1), cells(2)
    for q in range(4):
        fx[1, q] = 0.5 * (before[q] + after[q])

    def cells_1(k):
        one, two = cells(2 + 2 * k), cells(3 + 2 * k)
        for q in range(2):
            sums[8 + k, q, 0:24] = (one[2 * q] + one[2 * q + 1]) + (two[2 * q] + two[2 * q + 1])
            sums[8 + k, q, 24:32] = jnp.zeros((8, 128), F32)

    def faces_0(p):
        c, c_next, b = cells(p), cells(p + 1), source(p)
        if p % 2:
            cells_1((p - 3) // 2)
        gx, gz, gy, d = plane_faces(c, c_next, [fx[p - 1, q] for q in range(4)], 0.5, 1, last, begin)
        for q in range(4):
            fx[p, q], fy[p, q], fz[p, q], diag[p, q] = gx[q], gy[q], gz[q], d[q]
            inv = inverse(c[q], d[q])
            dinv[p, q] = inv
            b0[p, q] = b[q]
            first[p, q] = b[q] * inv * (1.0 / THETA)

    loop(2, 22, faces_0)

    def second_0(p):
        near = neighbours(first, fx, fz, fy, p, 4, 1)
        for q in range(4):
            x0[p, q] = (1.0 + KEEP - GAIN) * first[p, q] + GAIN * (b0[p, q] + near[q]) * dinv[p, q]

    loop(3, 21, second_0)

    def residual_0(k):
        total = [jnp.zeros((24, 128), F32)] * 2
        for p in (4 + 2 * k, 5 + 2 * k):
            near = neighbours(x0, fx, fz, fy, p, 4, 1)
            for q in range(4):
                total[q // 2] = total[q // 2] + (b0[p, q] + near[q] - diag[p, q] * x0[p, q])
        for q in range(2):
            sums[k, q, 0:24] = total[q]
            sums[k, q, 24:32] = jnp.zeros((8, 128), F32)

    loop(0, 8, residual_0)

    def halve(k, q):
        return 0.125 * (sums[k, q, pl.ds(0, 16, stride=2), :] + sums[k, q, pl.ds(1, 16, stride=2), :])

    for q in range(2):
        loop(0, 8, lambda k, q=q: b1.__setitem__((k + 1, q), halve(k, q)))
        loop(0, 10, lambda k, q=q: c1.__setitem__((k, q), halve(8 + k, q)))

    lane = iota((16, 128), 1)
    last_1, begin_1 = lane == 127, lane == 0
    for q in range(2):
        fx1[0, q] = 0.125 * (c1[0, q] + c1[1, q])

    def faces_1(p):
        c, c_next = [c1[p, q] for q in range(2)], [c1[p + 1, q] for q in range(2)]
        gx, gz, gy, d = plane_faces(c, c_next, [fx1[p - 1, q] for q in range(2)], 0.125, 1, last_1, begin_1)
        for q in range(2):
            fx1[p, q], fy1[p, q], fz1[p, q], diag1[p, q] = gx[q], gy[q], gz[q], d[q]
            inv = inverse(c[q], d[q])
            dinv1[p, q] = inv
            first1[p, q] = b1[p, q] * inv * (1.0 / THETA)

    loop(1, 9, faces_1)

    def second_1(p):
        near = neighbours(first1, fx1, fz1, fy1, p, 2, 1)
        for q in range(2):
            x1[p, q] = (1.0 + KEEP - GAIN) * first1[p, q] + GAIN * (b1[p, q] + near[q]) * dinv1[p, q]

    loop(2, 8, second_1)

    y, size = lax.axis_index("y"), lax.axis_size("n")
    for x in range(2):
        total = jnp.zeros((16, 128), F32)
        cell = jnp.zeros((16, 128), F32)
        for p in (3 + 2 * x, 4 + 2 * x):
            near = neighbours(x1, fx1, fz1, fy1, p, 2, 1)
            for q in range(2):
                rest = b1[p, q] + near[q] - diag1[p, q] * x1[p, q]
                r1[p, q] = rest
                total = total + rest
                cell = cell + c1[p, q]
                place = p - 3
                parts[place // 2, place % 2, 4 * q : 4 * q + 4] = rest[4:8]
                row = 4 * (place % 2) + 2 * q
                parts[2, place // 2, row : row + 2] = rest[6:8]
                parts[3, place // 2, row : row + 2] = rest[4:6]
        total = 0.125 * (total + shift(total, 1, 0))
        cell = 0.125 * (cell + shift(cell, 1, 0))
        for yy in range(2):
            packed[0, 2, 2 * x + yy : 2 * x + yy + 1] = total[4 + 2 * yy : 5 + 2 * yy]
            packed[0, 2, 4 + 2 * x + yy : 5 + 2 * x + yy] = cell[4 + 2 * yy : 5 + 2 * yy]

    level_two = packed[0, 2]
    for y_to in range(depth):
        ahead = (y_to - y + depth) % depth
        for n_to in range(size):
            beside = jnp.where(n_to > n, 2, 3)
            part = jnp.where(ahead == 0, beside, jnp.where(ahead == 1, 1, 0))
            s = y_to * size + n_to
            packed[s, 0] = parts[part, 0]
            packed[s, 1] = parts[part, 1]
            packed[s, 2] = level_two


def edge_kernel(plane, other, pair, *, depth):
    n = lax.axis_index("n")
    even = lax.axis_index("z") % 2 == 0
    size = lax.axis_size("n")

    count = (depth - 1) * size
    def send(s, up, down):
        pair[s] = jnp.where(even, up, down)
        other[s] = jnp.where(even, down, up)

    for s in range(count):
        send(s, plane[size + s, 2], plane[s, 2])
    for k in range(3):
        place = jnp.clip(n + (k - 1), 0, size - 1)
        for j in range(2):
            send(count + 2 * k + j, plane[count + place, j], plane[place, j])


def middle_kernel(plane, other, pair, r1, sent, x2, r2, fx, fy, fz, dinv, r1h, b2, c2, diag, first, half, *, depth, tall):
    z, y, n = lax.axis_index("z"), lax.axis_index("y"), lax.axis_index("n")
    size = lax.axis_size("n")
    even = z % 2 == 0

    def below(rows):
        return jnp.where(even, other[rows, :], pair[rows, :])

    def above(rows):
        return jnp.where(even, pair[rows, :], other[rows, :])

    width = 2 * depth
    for yb in range(depth):
        for x in range(2):
            for yy in range(2):
                r = 2 * x + yy
                place = 2 * yb + x
                own = yb * size * 24 + 16 + r
                b2[width + place, yy] = plane[pl.ds(own, 8, stride=24), :]
                c2[width + place, yy] = plane[pl.ds(own + 4, 8, stride=24), :]
                if yb > 0:
                    edge = (yb - 1) * size * 8 + r
                    b2[place, yy] = below(pl.ds(edge, 8, stride=8))
                    c2[place, yy] = below(pl.ds(edge + 4, 8, stride=8))
                if yb < depth - 1:
                    edge = yb * size * 8 + r
                    b2[2 * width + place, yy] = above(pl.ds(edge, 8, stride=8))
                    c2[2 * width + place, yy] = above(pl.ds(edge + 4, 8, stride=8))

    scale = 0.5 / 16.0
    shape = (8, 128)
    row, lane = iota(shape, 0), iota(shape, 1)
    last, begin, last_b, begin_b = row == 7, row == 0, lane == 127, lane == 0
    for q in range(2):
        fx[2, q] = scale * (c2[2, q] + c2[3, q])

    def faces_2(p):
        c, c_next = [c2[p, q] for q in range(2)], [c2[p + 1, q] for q in range(2)]
        gx, gy, gz, d = plane_faces(c, c_next, [fx[p - 1, q] for q in range(2)], scale, 0, last, begin, last_b, begin_b)
        for q in range(2):
            fx[p, q], fy[p, q], fz[p, q], diag[p, q] = gx[q], gy[q], gz[q], d[q]
            inv = inverse(c[q], d[q])
            dinv[p, q] = inv
            first[p, q] = b2[p, q] * inv * (1.0 / THETA)

    loop(3, 3 * width - 3, faces_2)

    def second_2(p):
        near = neighbours(first, fx, fy, fz, p, 2, 0)
        for q in range(2):
            x2[p, q] = (1.0 + KEEP - GAIN) * first[p, q] + GAIN * (b2[p, q] + near[q]) * dinv[p, q]

    loop(4, 3 * width - 4, second_2)

    totals = [jnp.zeros(shape, F32)] * depth
    cell_sums = [jnp.zeros(shape, F32)] * depth
    for p in range(5, 3 * width - 5):
        near = neighbours(x2, fx, fy, fz, p, 2, 0)
        j = (p - width) // 2
        for q in range(2):
            rest = b2[p, q] + near[q] - diag[p, q] * x2[p, q]
            r2[p, q] = rest
            if 0 <= j < depth:
                totals[j] = totals[j] + rest
                cell_sums[j] = cell_sums[j] + c2[p, q]
    zz, k = iota((128, 128), 0), iota((128, 128), 1)
    low_half = ones_where(k == zz // 2, 0.125)
    high_half = ones_where(k == zz // 2 + 64, 0.125)
    coarse = dot_exact(jnp.concatenate(totals, axis=0), low_half) + dot_exact(jnp.concatenate(cell_sums, axis=0), high_half)
    for j in range(depth):
        half[j // 2, j % 2] = coarse[8 * j : 8 * j + 8]
    mine = half[n % 2]
    for s in range(tall):
        sent[s] = mine

    for p in range(3, 7):
        for q in range(2):
            r1h[p, q] = r1[p, q]
    edges = 8 * (depth - 1) * size
    for k in range(3):
        place = jnp.clip(n + (k - 1), 0, size - 1)

        def block(yb, j):
            start = pl.multiple_of((yb * size + place) * 24 + 8 * j, 8)
            return plane[pl.ds(start, 8), :]

        for j in range(2):
            start = edges + 8 * (2 * k + j)
            low = jnp.where(y == 0, below(pl.ds(start, 8)), block(jnp.maximum(y - 1, 0), j))
            high = jnp.where(y == depth - 1, above(pl.ds(start, 8)), block(jnp.minimum(y + 1, depth - 1), j))
            for q in range(2):
                r1h[1 + j, q, 4 * k : 4 * k + 4] = low[4 * q : 4 * q + 4]
                r1h[7 + j, q, 4 * k : 4 * k + 4] = high[4 * q : 4 * q + 4]
                r1h[1 + j, q, 12:16] = jnp.zeros((4, 128), F32)
                r1h[7 + j, q, 12:16] = jnp.zeros((4, 128), F32)
            if k != 1:
                tile = block(y, j)
                start = 2 if k == 0 else 8
                for x in range(2):
                    for q in range(2):
                        row = 4 * x + 2 * q
                        r1h[3 + 2 * j + x, q, start : start + 2] = tile[row : row + 2]


def sweeps(start, mid, out, source, fx, fa, fb, dinv, low, planes, count, axis):
    def one(p):
        near = neighbours(start, fx, fa, fb, p, count, axis)
        for q in range(count):
            mid[p, q] = (1.0 - 1.0 / THETA) * start[p, q] + (1.0 / THETA) * ((source[p, q] + near[q]) * dinv[p, q])

    loop(-1, planes + 1, lambda k: one(low + k))

    def two(p):
        near = neighbours(mid, fx, fa, fb, p, count, axis)
        for q in range(count):
            value = (1.0 - GAIN + KEEP) * mid[p, q] - KEEP * start[p, q]
            out(p, q, value + GAIN * ((source[p, q] + near[q]) * dinv[p, q]))

    loop(0, planes, lambda k: two(low + k))


def up_kernel(gathered, r1h, x2, r2, fx2, fy2, fz2, dinv2, c1, x1, fx1, fy1, fz1, dinv1, x0, b0, fx, fy, fz, dinv, result,
              c3, p3, r3, x3, i3, fx3, fy3, fz3, d3, s2, m2, f2, s1, m1, f1, s0, m0, f0, *, depth, tall):
    z, y, n = lax.axis_index("z"), lax.axis_index("y"), lax.axis_index("n")
    half = depth * tall // 2
    shape = (8, 128)
    row, lane = iota(shape, 0), iota(shape, 1)
    upper = lane >= 64

    def unpack(i):
        one, two = [gathered[j % depth // 2, j // depth, j % 2] for j in (i, i + half)]
        b = jnp.where(upper, pltpu.roll(two, 64, 1), one)
        c3[i + 1, 0] = jnp.where(upper, two, pltpu.roll(one, 64, 1))
        r3[i + 1, 0] = b
        p3[i + 1, 0] = b
        x3[i + 1, 0] = jnp.zeros(shape, F32)

    loop(0, half, unpack)

    def wrap(ref):
        ref[0, 0] = jnp.where(upper, pltpu.roll(ref[half, 0], 64, 1), 0.0)
        ref[half + 1, 0] = jnp.where(upper, 0.0, pltpu.roll(ref[1, 0], 64, 1))

    wrap(c3)
    scale = 0.5 / 64.0
    fx3[0, 0] = scale * (c3[0, 0] + c3[1, 0])

    def faces_3(p):
        gx, gy, gz, d = plane_faces([c3[p, 0]], [c3[p + 1, 0]], [fx3[p - 1, 0]], scale, 0, row == 7, row == 0, lane % 64 == 63, lane % 64 == 0)
        fx3[p, 0], fy3[p, 0], fz3[p, 0], d3[p, 0] = gx[0], gy[0], gz[0], d[0]

    loop(1, half + 1, faces_3)

    def whole(parts):
        total = functools.reduce(lambda a, b: a + b, parts)
        return jnp.sum(jnp.sum(total, axis=0, keepdims=True), axis=1, keepdims=True)

    def spread(values):
        parts = [jnp.zeros(shape, F32)] * 4
        for i, value in enumerate(values):
            parts[i % 4] = parts[i % 4] + value
        return whole(parts)

    start_norm = spread([r3[i + 1, 0] * r3[i + 1, 0] for i in range(half)])

    def iterate(norm):
        wrap(p3)
        products = []
        for p in range(1, half + 1):
            here = p3[p, 0]
            image = d3[p, 0] * here - neighbours(p3, fx3, fy3, fz3, p, 1, 0)[0]
            i3[p, 0] = image
            products.append(here * image)
        alpha = norm / spread(products)
        squares = []
        for p in range(1, half + 1):
            x3[p, 0] = x3[p, 0] + alpha * p3[p, 0]
            rest = r3[p, 0] - alpha * i3[p, 0]
            r3[p, 0] = rest
            squares.append(rest * rest)
        new = spread(squares)
        beta = new / norm
        for p in range(1, half + 1):
            p3[p, 0] = r3[p, 0] + beta * p3[p, 0]
        return new

    norm = start_norm
    for _ in range(COARSE_SWEEPS):
        norm = iterate(norm)

    base = 2 * depth + 2 * y - 4
    tiles = []
    for j in range(5):
        place = jnp.clip(depth * z + y - 2 + j, 0, 2 * half - 1)
        high = place >= half
        tile = x3[jnp.where(high, place - half, place) + 1, 0]
        tiles.append(jnp.where(high, pltpu.roll(tile, 64, 1), tile))
    k, zz = iota((128, 128), 0), iota((128, 128), 1)
    fine = dot_exact(jnp.concatenate(tiles, axis=0), ones_where(k == zz // 2))
    for j in range(5):
        add = fine[8 * j : 8 * j + 8]
        for p in (base + 2 * j, base + 2 * j + 1):
            for q in range(2):
                s2[p, q] = jnp.where(dinv2[p, q] > 0.0, add, 0.0)

    def keep_2(p, q, value):
        f2[p, q] = x2[p, q] + value

    sweeps(s2, m2, keep_2, r2, fx2, fy2, fz2, dinv2, base + 2, 6, 2, 0)

    wide = jnp.concatenate([jnp.concatenate([f2[base + 2 + k, 0], f2[base + 2 + k, 1]], axis=0) for k in range(6)], axis=1)
    r, k = iota((16, 16), 0), iota((16, 16), 1)
    from_n = n + r // 4 - 1
    pick = ones_where((k == (r // 2) % 2 * 8 + from_n) & (from_n >= 0) & (from_n < 8))
    fine = chosen_dot(pick, wide)
    for p in range(10):
        k = (p + 1) // 2
        for q in range(2):
            s1[p, q] = jnp.where(c1[p, q] > 0.0, fine[:, 128 * k : 128 * k + 128], 0.0)

    def keep_1(p, q, value):
        f1[p, q] = x1[p, q] + value

    sweeps(s1, m1, keep_1, r1h, fx1, fz1, fy1, dinv1, 2, 6, 2, 1)

    wide = jnp.concatenate([f1[p, q] for p in range(2, 8) for q in range(2)], axis=1)
    r, k = iota((24, 16), 0), iota((24, 16), 1)
    fine = chosen_dot(ones_where(k == r // 2), wide)
    for p in range(6, 18):
        for q in range(4):
            j = 2 * (p // 2 - 3) + q // 2
            s0[p, q] = jnp.where(dinv[p, q] > 0.0, x0[p, q] + fine[:, 128 * j : 128 * j + 128], 0.0)

    def keep_0(p, q, value):
        start = (p - 8) * 8
        if not isinstance(start, int):
            start = pl.multiple_of(start, 8)
        f0[pl.ds(start, 8), 128 * q : 128 * q + 128] = value[8:16]

    sweeps(s0, m0, keep_0, b0, fx, fz, fy, dinv, 8, 8, 4, 1)
    k, z0 = iota((512, 512), 0), iota((512, 512), 1)
    back = ones_where(z0 == 4 * (k % 128) + k // 128)
    result[...] = dot_exact(f0[...], back).reshape(8, 8, 512)


def call(kernel, outs, *operands, scratch=(), limit=40):
    shapes = [jax.ShapeDtypeStruct(shape, F32) for shape in outs]
    return pl.pallas_call(
        kernel,
        out_shape=shapes,
        in_specs=[pl.BlockSpec(memory_space=pltpu.VMEM)] * len(operands),
        out_specs=[pl.BlockSpec(memory_space=pltpu.VMEM)] * len(outs),
        scratch_shapes=[pltpu.VMEM(shape, F32) for shape in scratch],
        compiler_params=pltpu.CompilerParams(vmem_limit_bytes=limit * 2**20),
    )(*operands)


def split(rhs_field, beta_cells):
    outs = [(16, 4, 8, 128), (SENT, 4, 8, 128), (SENT, 4, 8, 128)]
    return pl.pallas_call(
        split_kernel,
        out_shape=[jax.ShapeDtypeStruct(shape, F32) for shape in outs],
        in_specs=[pl.BlockSpec(memory_space=pltpu.HBM)] * 2,
        out_specs=[pl.BlockSpec(memory_space=pltpu.VMEM)] * 3,
        scratch_shapes=[pltpu.VMEM((8, 8, 512), F32)] * 2 + [pltpu.SemaphoreType.DMA((2,))],
        compiler_params=pltpu.CompilerParams(vmem_limit_bytes=40 * 2**20),
    )(pltpu.with_memory_space_constraint(rhs_field, pltpu.HBM), pltpu.with_memory_space_constraint(beta_cells, pltpu.HBM))


def ring(axis_size, step):
    return [(i, (i + step) % axis_size) for i in range(axis_size)]


def pairs(axis_size):
    return [(i, i ^ 1) for i in range(axis_size)]


def others(axis_size):
    return [(i, ((i + 1) ^ 1) - 1) for i in range(1, axis_size - 1)]


def shards(rhs_field, beta_cells):
    tall, depth, size = lax.axis_size("z"), lax.axis_size("y"), lax.axis_size("n")
    wide, group = tall * depth, depth * size
    own, to_pair, to_other = split(rhs_field, beta_cells)
    own_left = lax.ppermute(own, "n", ring(size, 1))
    own_right = lax.ppermute(own, "n", ring(size, -1))
    other = lax.ppermute(to_other, ("z", "y"), others(wide))
    pair = lax.ppermute(to_pair, ("z", "y"), pairs(wide))
    corners = []
    for planes in (pair, other):
        to_right, to_left = call(corner_kernel, [(len(CORNERS), 4, 8, 128)] * 2, planes)
        corners += [lax.ppermute(to_right, "n", ring(size, 1)), lax.ppermute(to_left, "n", ring(size, -1))]
    fine, coarse = (24, 4, 24, 128), (10, 2, 16, 128)
    outs = call(
        functools.partial(down_kernel, depth=depth),
        [(group, 3, 8, 128)] + [fine] * 6 + [coarse] * 7,
        own, pair, other, own_left, own_right, *corners,
        scratch=[fine, fine, (18, 2, 32, 128), coarse, coarse, coarse, (4, 2, 8, 128)],
    )
    packed, level_zero = outs[0], outs[1:7]
    c1, x1, r1, *faces_1 = outs[7:14]
    plane = lax.all_to_all(packed, ("y", "n"), 0, 0)
    edge = group - size + 6
    to_other, to_pair = call(functools.partial(edge_kernel, depth=depth), [(edge, 8, 128)] * 2, plane)
    other = lax.ppermute(to_other, "z", others(tall))
    pair = lax.ppermute(to_pair, "z", pairs(tall))
    slab = (6 * depth, 2, 8, 128)
    outs = call(
        functools.partial(middle_kernel, depth=depth, tall=tall),
        [(tall, depth // 2, 8, 128)] + [slab] * 6 + [coarse],
        plane.reshape(group * 24, 128), other.reshape(edge * 8, 128), pair.reshape(edge * 8, 128), r1,
        scratch=[slab, slab, slab, slab, (2, depth // 2, 8, 128)],
    )
    sent, level_two, r1h = outs[0], outs[1:7], outs[7]
    gathered = lax.all_to_all(sent, "z", 0, 0)
    cores = [[2 * i, 2 * i + 1] for i in range(size // 2)]
    gathered = lax.all_gather(gathered, "n", axis_index_groups=cores)
    packed_3 = (wide // 2 + 2, 1, 8, 128)
    (result,) = call(
        functools.partial(up_kernel, depth=depth, tall=tall),
        [(8, 8, 512)],
        gathered, r1h, *level_two, c1, x1, *faces_1, *level_zero,
        scratch=[packed_3] * 9 + [slab] * 3 + [coarse] * 3 + [fine] * 2 + [(64, 512)],
    )
    return result


def solution(mesh):
    wide, size = mesh.shape["wide"], mesh.shape["narrow"]
    inner = Mesh(mesh.devices.reshape(wide // 4, 4, size), ("z", "y", "n"))
    spec = P(("z", "y"), "n", None)
    return jax.shard_map(shards, mesh=inner, in_specs=(spec, spec), out_specs=spec, check_vma=False)
```
